32 devices in a mesh: grp: 4 (over x, core), ep: 8 (over z, y).
Axes of the slice: x: 2, y: 2, z: 4, core: 2. Of those that a mesh axis runs over, the one named last changes fastest.
Arguments:
- tokens: bfloat16 [2, 4, 512, 2048], P(None, 'grp', 'ep'), may hold values from -6 to 6
- routes: int32 [2, 4, 512, 8], P(None, 'grp', 'ep'), may hold values from 0 to 15, all different within a row; in each aligned block of 64 rows (0 to 63, 64 to 127, ..., all dimensions but the last counted through in order) at most 36 rows name the same one
- attn_gain: bfloat16 [2048], P(('grp', 'ep')), may hold values from 0.5 to 1.5
- w_query: bfloat16 [2048, 2048], P(('grp', 'ep')), may hold values from -0.125 to 0.125
- w_key: bfloat16 [2048, 2048], P(('grp', 'ep')), may hold values from -0.125 to 0.125
- w_value: bfloat16 [2048, 2048], P(('grp', 'ep')), may hold values from -0.125 to 0.125
- query_gain: bfloat16 [2048], P(('grp', 'ep')), may hold values from 0.5 to 1.5
- key_gain: bfloat16 [2048], P(('grp', 'ep')), may hold values from 0.5 to 1.5
- w_out: bfloat16 [2048, 2048], P(('grp', 'ep')), may hold values from -0.75 to 0.75
- moe_gain: bfloat16 [2048], P(('grp', 'ep')), may hold values from 0.5 to 1.5
- w_router: bfloat16 [2048, 16], P(('grp', 'ep')), may hold values from -0.0625 to 0.0625
- w_gate: bfloat16 [16, 2048, 1024], P('ep'), may hold values from -0.125 to 0.125
- w_up: bfloat16 [16, 2048, 1024], P('ep'), may hold values from -0.125 to 0.125
- w_down: bfloat16 [16, 1024, 2048], P('ep'), may hold values from -1.5 to 1.5
- cotangent: bfloat16 [2, 4, 512, 2048], P(None, 'grp', 'ep'), may hold values from -6 to 6
Outputs:
- block_out: bfloat16 [2, 4, 512, 2048], P(None, 'grp', 'ep')
- d_tokens: float32 [2, 4, 512, 2048], P(None, 'grp', 'ep')
- d_attn_gain: float32 [2048], P(('grp', 'ep'))
- d_query: float32 [2048, 2048], P(('grp', 'ep'))
- d_key: float32 [2048, 2048], P(('grp', 'ep'))
- d_value: float32 [2048, 2048], P(('grp', 'ep'))
- d_query_gain: float32 [2048], P(('grp', 'ep'))
- d_key_gain: float32 [2048], P(('grp', 'ep'))
- d_out: float32 [2048, 2048], P(('grp', 'ep'))
- d_moe_gain: float32 [2048], P(('grp', 'ep'))
- d_router: float32 [2048, 16], P(('grp', 'ep'))
- d_gate: float32 [16, 2048, 1024], P('ep')
- d_up: float32 [16, 2048, 1024], P('ep')
- d_down: float32 [16, 1024, 2048], P('ep')
The draws below stay inside these ranges and needn't reach their ends.
Inputs may be any that keep to these rules, and one draw needn't show every extreme that they name: `routes`: each token names 8 different experts. In each micro-batch the 64 tokens of one device name no expert more than 36 times.
All inputs are finite; a program needn't handle non-finite values.
Results may differ from the reference program's by a relative error of at most 0.02.
Values may be sent and summed in bfloat16 or wider, within the bound.
No kernel may reach another device: no remote copies, remote signals or barrier semaphores. Data moves between devices by JAX's collectives and lax.ppermute only.
A program may use at most 384 MiB of HBM per device.

```python
import math
import jax
import jax.numpy as jnp
import numpy as np
from jax import lax

D = 2048
HEADS = 16
FF = 1024
EXPERTS = 16
TOP = 8
MICRO = 2
MB_TOK = 64
SEQ = 512
SEQS = 4
CAP = 36


def strengthened(values, key, source, target, blocks, factor):
    owner, partner = [(jnp.arange(values.shape[axis_at]) // (values.shape[axis_at] // blocks)).reshape([-1 if axis == axis_at else 1 for axis in range(values.ndim)]) for axis_at in (source, target)]
    chosen = jax.random.permutation(key, blocks)[partner]
    strong = (owner == chosen) | (owner == (partner + blocks // 2) % blocks)
    return jnp.where(strong, factor * values, values)


def levels(stream_key, dims, split, low, largest):
    gain = 1.0
    for axis_at, shards_of in split:
        heights = jax.random.uniform(jax.random.fold_in(jax.random.fold_in(stream_key, 6), axis_at), (shards_of,), jnp.float32, low / len(split), largest / len(split))
        gain = gain * jnp.repeat(jnp.exp(heights), dims[axis_at] // shards_of).reshape((-1,) + (1,) * (len(dims) - 1 - axis_at))
    return gain


def deal_out(rng, own, number, rows, count, top, limit, lean):
    ranking = jax.random.permutation(rng, count)
    crowded, ordinary = load_shares(count, rows * top, limit, lean, True), load_shares(count, rows * top, limit, lean, False)
    places = jnp.arange(count)

    def named(lengths, rotation):
        used = int((lengths > 0).sum())
        fixed = max(1, used // 4)
        moved = fixed + (places - fixed + rotation * (used - fixed)) % max(1, count - fixed)
        return jnp.zeros((count,), jnp.int32).at[ranking[jnp.where(places < fixed, places, moved)]].set(jnp.asarray(lengths, jnp.int32))

    lengths = jnp.where(number % 4 == 0, named(crowded, number // 4), named(ordinary, number - number // 4 - 1))
    mixed = jax.random.permutation(jax.random.fold_in(own, 3), count)
    giver, receiver = mixed[0:count // 2 * 2:2], mixed[1:count // 2 * 2:2]
    slack = jnp.minimum(lengths[giver] - 1, limit - lengths[receiver]) // 2
    slack = jnp.where((giver == ranking[0]) | (receiver == ranking[0]) | (lengths[receiver] == 0), 0, jnp.maximum(slack, 0))
    moved = jax.random.randint(jax.random.fold_in(own, 4), (count // 2,), 0, 1 << 20) % (slack + 1)
    lengths = lengths.at[giver].add(-moved).at[receiver].add(moved)
    members = jnp.searchsorted(jnp.cumsum(lengths), jnp.arange(rows * top), side="right").astype(jnp.int32)
    listing = members.reshape(top, rows).T
    listing = listing[jax.random.permutation(jax.random.fold_in(own, 1), rows)]
    rotation = jax.random.randint(jax.random.fold_in(own, 2), (rows, 1), 0, top)
    return jnp.take_along_axis(listing, (jnp.arange(top)[None, :] + rotation) % top, axis=1)


def load_shares(number_of, total, bound, lean, full):
    portions = [(1 << 20) // math.isqrt(grade ** lean) + 1 for grade in range(1, number_of + 1)]
    largest = bound if full else min(bound, max(-(-total // number_of), total * portions[0] // sum(portions)))
    least = 1 if total - largest >= number_of - 1 else 0
    counts, rest = [largest] + [least] * (number_of - 1), total - largest - least * (number_of - 1)
    while rest > 0:
        candidates = [i for i in range(1, number_of) if counts[i] < largest] or [i for i in range(1, number_of) if counts[i] < bound]
        pool, remaining = sum([portions[i] for i in candidates]), rest
        for i in candidates:
            more = min(bound - counts[i], max(1, remaining * portions[i] // pool), rest)
            counts[i] = counts[i] + more
            rest = rest - more
    return np.array(counts)


def bell_draw(rng, shape, spread, bound, cuts=(), kind=jnp.bfloat16):
    gain = levels(rng, shape, cuts, -0.22, 0.18) if cuts else 1.0
    entries = jax.random.normal(rng, shape, jnp.float32) * spread * gain
    return jnp.minimum(jnp.maximum(entries, -bound), bound).astype(kind)


def heavy_noise(key, dims, deviation, bound, split, heavy, held_as=jnp.bfloat16):
    values = deviation * jax.random.normal(key, dims, jnp.float32)
    if split:
        values = values * levels(key, dims, split, -0.22, 0.18)
    return jnp.clip(strengthened(values, jax.random.fold_in(key, 3), *heavy), -bound, bound).astype(held_as)


def setup_inputs(seed: int = 0) -> dict:
    keys = jax.random.split(jax.random.key(seed), 16)
    tokens = heavy_noise(keys[0], (MICRO, SEQS, SEQ, D), 1.0, 6.0, ((1, 4), (2, 8)), (2, 3, 8, 2.0))
    routes_keys = jax.random.split(jax.random.fold_in(keys[1], 1), MICRO * SEQS * SEQ // MB_TOK)
    routes_turns = jax.random.permutation(jax.random.fold_in(keys[1], 3), MICRO * SEQS * SEQ // MB_TOK)
    routes = jax.vmap(lambda own, number: deal_out(jax.random.fold_in(keys[1], 2), own, number, MB_TOK, EXPERTS, TOP, CAP, 1))(routes_keys, routes_turns).reshape((MICRO, SEQS, SEQ, TOP))
    attn_gain = jnp.clip(1.0 + 0.1 * jax.random.normal(keys[2], (D,), jnp.float32), 0.5, 1.5).astype(jnp.bfloat16)
    w_query = bell_draw(keys[3], (D, D), D ** -0.5, 0.125, ((0, 32),))
    w_key = bell_draw(keys[4], (D, D), D ** -0.5, 0.125, ((0, 32),))
    w_value = bell_draw(keys[5], (D, D), D ** -0.5, 0.125, ((0, 32),))
    query_gain = jnp.clip(1.0 + 0.1 * jax.random.normal(keys[6], (D,), jnp.float32), 0.5, 1.5).astype(jnp.bfloat16)
    key_gain = jnp.clip(1.0 + 0.1 * jax.random.normal(keys[7], (D,), jnp.float32), 0.5, 1.5).astype(jnp.bfloat16)
    w_out = bell_draw(keys[8], (D, D), (D // 32) ** -0.5, 0.75, ((0, 32),))
    moe_gain = jnp.clip(1.0 + 0.1 * jax.random.normal(keys[9], (D,), jnp.float32), 0.5, 1.5).astype(jnp.bfloat16)
    w_router = bell_draw(keys[10], (D, EXPERTS), (4 * D) ** -0.5, 0.0625, ((0, 32),))
    w_gate = bell_draw(keys[11], (EXPERTS, D, FF), D ** -0.5, 0.125, ((0, 8),))
    w_up = bell_draw(keys[12], (EXPERTS, D, FF), D ** -0.5, 0.125, ((0, 8),))
    w_down = bell_draw(keys[13], (EXPERTS, FF, D), (max(FF // 64, 1)) ** -0.5, 1.5, ((0, 8),))
    cotangent = bell_draw(keys[14], (MICRO, SEQS, SEQ, D), 1.0, 6.0, ((1, 4), (2, 8)))
    return dict(tokens=tokens, routes=routes, attn_gain=attn_gain, w_query=w_query, w_key=w_key, w_value=w_value, query_gain=query_gain, key_gain=key_gain, w_out=w_out, moe_gain=moe_gain, w_router=w_router, w_gate=w_gate, w_up=w_up, w_down=w_down, cotangent=cotangent)


NORM_EPSILON = 1e-05
ROPE_BASE = 10000.0

@jax.custom_vjp
def low(v):
    return lax.optimization_barrier(v.astype(jnp.bfloat16)).astype(jnp.float32)

@jax.custom_vjp
def low_back(v):
    return v

def low_keep(v):
    return (low(v), None)

def low_pass(kept, grad):
    return (grad,)

def back_keep(v):
    return (v, None)

def back_low(kept, grad):
    return (low(grad),)
low.defvjp(low_keep, low_pass)
low_back.defvjp(back_keep, back_low)

def product(left, right):
    return jnp.dot(left, right, precision=lax.Precision.HIGHEST, preferred_element_type=jnp.float32)

def rms_scale(values, gain_vec):
    return values * lax.rsqrt(lax.optimization_barrier(jnp.mean(values * values, axis=-1, keepdims=True)) + NORM_EPSILON) * gain_vec

def rotary(values, positions):
    half_dim = values.shape[-1] // 2
    frequency = jnp.exp(-math.log(ROPE_BASE) * jnp.arange(half_dim, dtype=jnp.float32) * 2.0 / values.shape[-1])
    angles = positions.astype(jnp.float32)[:, None] * frequency[None, :]
    cosine = jnp.cos(angles)[:, None, :]
    sine_part = jnp.sin(angles)[:, None, :]
    first_half = values[..., :half_dim]
    second = values[..., half_dim:]
    return jnp.concatenate([first_half * cosine - second * sine_part, second * cosine + first_half * sine_part], axis=-1)

def prepare(raw_rows, gain_vec, positions):
    normed = rms_scale(raw_rows, gain_vec)
    shaped = normed.reshape(raw_rows.shape[0], HEADS, raw_rows.shape[1] // HEADS)
    return rotary(shaped, positions).reshape(raw_rows.shape)

def attend(query_low, key_low, value_low):
    length = query_low.shape[0]
    head_dim = D // HEADS
    query_heads = query_low.reshape(length, HEADS, head_dim)
    key_heads = key_low.reshape(length, HEADS, head_dim)
    value_heads = value_low.reshape(length, HEADS, head_dim)
    scores = jnp.einsum('qhd,khd->hqk', query_heads, key_heads, precision=lax.Precision.HIGHEST) * (1.0 / math.sqrt(head_dim))
    places = jnp.arange(length, dtype=jnp.int32)
    allowed = places[:, None] >= places[None, :]
    scores = low_back(jnp.where(allowed[None, :, :], scores, -1e+30))
    attn_probs = jax.nn.softmax(scores, axis=-1)
    attended = jnp.einsum('hqk,khd->qhd', low(attn_probs), value_heads, precision=lax.Precision.HIGHEST)
    return attended.reshape(length, D)

@jax.checkpoint
def attend_parts(pieces):
    return attend(pieces[0], pieces[1], pieces[2])

def experts(moe_in, route_ids, w_gate, w_up, w_down):
    pair_count = route_ids.shape[0] * route_ids.shape[1]
    flat_route = route_ids.reshape(-1)
    member = (flat_route[:, None] == jnp.arange(EXPERTS, dtype=jnp.int32)[None, :]).astype(jnp.int32)
    slot_rank = lax.optimization_barrier(jnp.sum((jnp.cumsum(member, axis=0) - member) * member, axis=1))
    expert_room = route_ids.shape[0]
    slot_index = (flat_route * expert_room + slot_rank).astype(jnp.int32)
    pair_rows = low_back(jnp.broadcast_to(moe_in[:, None, :], (route_ids.shape[0], route_ids.shape[1], D)).reshape(pair_count, D))
    buffer = jnp.zeros((EXPERTS * expert_room, D), pair_rows.dtype).at[slot_index].set(pair_rows).reshape(EXPERTS, expert_room, D)
    gate_pre = low_back(jnp.einsum('erd,edf->erf', buffer, w_gate, precision=lax.Precision.HIGHEST))
    up_pre = low_back(jnp.einsum('erd,edf->erf', buffer, w_up, precision=lax.Precision.HIGHEST))
    activation = low(jax.nn.silu(gate_pre) * up_pre)
    rows_out = low(low_back(jnp.einsum('erf,efd->erd', activation, w_down, precision=lax.Precision.HIGHEST)))
    return rows_out.reshape(EXPERTS * expert_room, D)[slot_index].reshape(route_ids.shape[0], route_ids.shape[1], D)

def forward_layer(tokens, routes, attn_gain, w_query, w_key, w_value, query_gain, key_gain, w_out, moe_gain, w_router, w_gate, w_up, w_down):
    results = []
    seq_count = tokens.shape[1]
    seq_len = tokens.shape[2]
    for micro_index in range(MICRO):
        resid_in = tokens[micro_index].reshape(seq_count * seq_len, D)
        route_ids = routes[micro_index].reshape(seq_count * seq_len, TOP)
        row_count = resid_in.shape[0]
        positions = jnp.arange(row_count, dtype=jnp.int32) % seq_len
        normed = low(rms_scale(resid_in, attn_gain))
        query_raw = low_back(product(normed, w_query))
        key_raw = low_back(product(normed, w_key))
        value_low = low(low_back(product(normed, w_value)))
        query_low = low(prepare(query_raw, query_gain, positions))
        key_low = low(prepare(key_raw, key_gain, positions))
        attended = lax.map(attend_parts, (query_low.reshape(seq_count, seq_len, D), key_low.reshape(seq_count, seq_len, D), value_low.reshape(seq_count, seq_len, D)))
        attended = low(low_back(attended.reshape(row_count, D)))
        resid_mid = resid_in + low_back(product(attended, w_out))
        moe_in = low(rms_scale(resid_mid, moe_gain))
        router_probs = jax.nn.softmax(low_back(product(moe_in, w_router)), axis=-1)
        gate_weights = jnp.take_along_axis(router_probs, route_ids, axis=1)
        expert_rows = experts(moe_in, route_ids, w_gate, w_up, w_down)
        mixed = resid_mid + lax.optimization_barrier(jnp.sum(gate_weights[:, :, None] * expert_rows, axis=1))
        results.append(mixed.reshape(seq_count, seq_len, D))
    return jnp.stack(results)

def reference(tokens, routes, attn_gain, w_query, w_key, w_value, query_gain, key_gain, w_out, moe_gain, w_router, w_gate, w_up, w_down, cotangent):
    floats = tuple((source.astype(jnp.float32) for source in (tokens, attn_gain, w_query, w_key, w_value, query_gain, key_gain, w_out, moe_gain, w_router, w_gate, w_up, w_down)))

    def forward(*values):
        return forward_layer(values[0], routes, *values[1:])
    result, pullback = jax.vjp(forward, *floats)
    gradients = pullback(cotangent.astype(jnp.float32))
    return (result.astype(jnp.bfloat16), gradients[0], gradients[1], gradients[2], gradients[3], gradients[4], gradients[5], gradients[6], gradients[7], gradients[8], gradients[9], gradients[10], gradients[11], gradients[12])
```

```python
import math

import jax
import jax.numpy as jnp
from jax import lax
from jax.sharding import Mesh, PartitionSpec as P

HEADS = 16
CAP = 36
NORM_EPSILON = 1e-05
ROPE_BASE = 10000.0
ALL = ("x", "core", "z", "y")
SWAP = ((0, 1), (1, 0))
F32 = jnp.float32
BF16 = jnp.bfloat16


def turn(count, step):
    return tuple((i, (i + step) % count) for i in range(count))


def mm(left, right):
    return jnp.dot(left, right, preferred_element_type=F32)


def mm_rows(left, right):
    return lax.dot_general(left, right, (((0,), (0,)), ((), ())), preferred_element_type=F32)


def mm_cols(left, right):
    return lax.dot_general(left, right, (((1,), (1,)), ((), ())), preferred_element_type=F32)


def unturn(items, index):
    count = len(items)
    if count == 1:
        return items
    placed = []
    for place in range(count):
        chosen = items[(0 - place) % count]
        for at in range(1, count):
            chosen = jnp.where(index == at, items[(at - place) % count], chosen)
        placed.append(chosen)
    return placed


def gather_ep(block, z_count, y_count):
    rows = []
    for k in range(z_count):
        along = block if k == 0 else lax.ppermute(block, "z", turn(z_count, k))
        for j in range(y_count):
            rows.append(along if j == 0 else lax.ppermute(along, "y", turn(y_count, j)))
    return jnp.concatenate(rows, axis=0)


def scatter_ep(part, z_count, y_count):
    rows = part.shape[0] // (z_count * y_count)
    low = part.astype(BF16)

    def piece(source, k, j):
        at = (k * y_count + j) * rows
        return source[at : at + rows]

    total = None
    for k in list(range(1, z_count)) + [0]:
        along = piece(part, k, 0).astype(F32)
        for j in range(1, y_count):
            along = along + lax.ppermute(piece(low, k, j), "y", turn(y_count, -j)).astype(F32)
        if k:
            along = lax.ppermute(along.astype(BF16), "z", turn(z_count, -k)).astype(F32)
        total = along if total is None else total + along
    return total


def sum_ep(values, z_count, y_count):
    shape = values.shape
    values = values.reshape(shape[0], z_count, y_count, -1)
    along = values
    for j in range(1, y_count):
        along = along + jnp.roll(lax.ppermute(values, "y", turn(y_count, j)), j, axis=2)
    total = along
    for k in range(1, z_count):
        total = total + jnp.roll(lax.ppermute(along, "z", turn(z_count, k)), k, axis=1)
    return total.reshape(shape)


def gather_grp(block, x_count):
    x_at, core = lax.axis_index("x"), lax.axis_index("core")
    mine = [block] + [lax.ppermute(block, "x", turn(x_count, i)) for i in range(1, x_count)]
    theirs = [lax.ppermute(item, "core", SWAP) for item in mine]
    mine, theirs = unturn(mine, x_at), unturn(theirs, x_at)
    stacked = []
    for own, other in zip(mine, theirs):
        stacked += [jnp.where(core == 0, own, other), jnp.where(core == 0, other, own)]
    return jnp.stack(stacked)


def scatter_grp(parts, x_count):
    x_at, core = lax.axis_index("x"), lax.axis_index("core")
    parts = parts.reshape((x_count, 2) + parts.shape[1:])
    away = lax.dynamic_index_in_dim(parts, 1 - core, 1, keepdims=False).astype(BF16)
    kept = lax.dynamic_index_in_dim(parts, core, 1, keepdims=False)
    kept = kept + lax.ppermute(away, "core", SWAP).astype(F32)
    total = lax.dynamic_index_in_dim(kept, x_at, 0, keepdims=False)
    for i in range(1, x_count):
        away = lax.dynamic_index_in_dim(kept, (x_at - i) % x_count, 0, keepdims=False)
        total = total + lax.ppermute(away.astype(BF16), "x", turn(x_count, -i)).astype(F32)
    return total


def norm_scale(values):
    return lax.rsqrt(jnp.mean(values * values, axis=-1, keepdims=True) + NORM_EPSILON)


def make_per_device(x_count, z_count, y_count):
    group_size = z_count * y_count
    grp_size = 2 * x_count

    def per_device(
        tokens,
        routes,
        attn_gain,
        w_query,
        w_key,
        w_value,
        query_gain,
        key_gain,
        w_out,
        moe_gain,
        w_router,
        w_gate,
        w_up,
        w_down,
        cotangent,
    ):
        micro_count, seq_parts, row_count, width = tokens.shape
        top_count = routes.shape[3]
        tokens = tokens.reshape(micro_count, row_count, width)
        routes = routes.reshape(micro_count, row_count, top_count)
        cotangent = cotangent.reshape(micro_count, row_count, width)
        expert_count = w_router.shape[1]
        seq_len = row_count * group_size
        head_dim = width // HEADS
        half = head_dim // 2
        score_scale = 1.0 / math.sqrt(head_dim)
        weight_rows = w_query.shape[0]
        pieces = head_dim // weight_rows
        heads_here = grp_size // pieces
        head_sets = group_size // pieces
        local_width = heads_here * head_dim
        x_at, core = lax.axis_index("x"), lax.axis_index("core")
        z_at, y_at = lax.axis_index("z"), lax.axis_index("y")
        ep_at = z_at * y_count + y_at
        set_at, piece_at = ep_at // pieces, ep_at % pieces
        slots = CAP * group_size
        local_experts = w_gate.shape[0]
        ff_width = w_gate.shape[2]

        def gather(block):
            return gather_ep(block, z_count, y_count)

        def scatter(part):
            return scatter_ep(part, z_count, y_count)

        small = jnp.concatenate(
            [w_router]
            + [g[:, None] for g in (attn_gain, query_gain, key_gain, moe_gain)],
            axis=1,
        )
        small = lax.all_gather(small, ALL, axis=0, tiled=True)
        full_router = small[:, :expert_count]
        gains = small[:, expert_count:].astype(F32).T
        gain_attn, gain_query, gain_key, gain_moe = gains[0:1], gains[1], gains[2], gains[3:4]

        def head_part(vector):
            shaped = vector.reshape(pieces, heads_here, head_sets, head_dim)
            shaped = lax.dynamic_index_in_dim(shaped, piece_at, 0, keepdims=False)
            return lax.dynamic_index_in_dim(shaped, set_at, 1, keepdims=False).reshape(1, -1)

        def head_part_back(vector):
            piece_hot = jnp.arange(pieces) == piece_at
            set_hot = jnp.arange(head_sets) == set_at
            hot = piece_hot[:, None, None, None] & set_hot[None, None, :, None]
            return jnp.where(hot, vector.reshape(1, heads_here, 1, head_dim), 0.0).reshape(-1)

        gain_query, gain_key = head_part(gain_query), head_part(gain_key)

        def by_owner(weight):
            shaped = weight.reshape(weight_rows, pieces, heads_here, head_sets, head_dim)
            return shaped.transpose(3, 1, 0, 2, 4).reshape(group_size, weight_rows, local_width)

        qkv = jnp.concatenate([by_owner(w) for w in (w_query, w_key, w_value)], axis=2)
        qkv = lax.all_to_all(qkv, ("z", "y"), split_axis=0, concat_axis=0, tiled=True)
        qkv = gather_grp(qkv.reshape(group_size * weight_rows, 3 * local_width), x_count)
        qkv = qkv.reshape(width, 3 * local_width)
        out_pairs = []
        for s in range(head_sets):
            for t in range(pieces):
                for h in range(heads_here):
                    for p in range(pieces):
                        home = (t * heads_here + h) * group_size + s * pieces + p
                        user = (h * pieces + p) * group_size + s * pieces + t
                        out_pairs.append((home, user))
        out_here = lax.ppermute(w_out, ALL, out_pairs)
        out_here = gather_grp(out_here, x_count).reshape(local_width, width)

        z_from = (z_at - jnp.arange(z_count, dtype=jnp.int32)) % z_count
        y_from = (y_at - jnp.arange(y_count, dtype=jnp.int32)) % y_count
        block_from = z_from[:, None] * y_count + y_from[None, :]
        positions = (
            block_from.reshape(-1)[:, None] * row_count
            + jnp.arange(row_count, dtype=jnp.int32)[None, :]
        ).reshape(-1)
        frequency = jnp.exp(
            -math.log(ROPE_BASE) * jnp.arange(half, dtype=F32) * 2.0 / head_dim
        )
        angles = positions.astype(F32)[:, None] * frequency[None, :]
        cosine, sine = jnp.cos(angles), jnp.sin(angles)
        cos_both = jnp.concatenate([cosine, cosine], axis=1)
        sin_both = jnp.concatenate([-sine, sine], axis=1)
        allowed = positions[:, None] >= positions[None, :]

        def halves_swapped(values):
            parts = []
            for h in range(heads_here):
                at = h * head_dim
                parts += [values[:, at + half : at + head_dim], values[:, at : at + half]]
            return jnp.concatenate(parts, axis=1)

        wide_cos = jnp.concatenate([cos_both] * heads_here, axis=1)
        wide_sin = jnp.concatenate([sin_both] * heads_here, axis=1)

        def rope(values):
            return values * wide_cos + halves_swapped(values) * wide_sin

        def rope_back(values):
            return values * wide_cos - halves_swapped(values) * wide_sin

        if local_experts == 2:
            expert_at = ep_at * 2 + core
            gate_w = lax.dynamic_index_in_dim(w_gate, core, 0, keepdims=False)
            up_w = lax.dynamic_index_in_dim(w_up, core, 0, keepdims=False)
            down_w = lax.dynamic_index_in_dim(w_down, core, 0, keepdims=False)
        else:
            assert local_experts == 1
            expert_at = ep_at
            part = ff_width // 2
            gate_w = lax.dynamic_slice_in_dim(w_gate[0], core * part, part, 1)
            up_w = lax.dynamic_slice_in_dim(w_up[0], core * part, part, 1)
            down_w = lax.dynamic_slice_in_dim(w_down[0], core * part, part, 0)
        expert_hot = jnp.arange(expert_count, dtype=jnp.int32) == expert_at

        named = lax.all_gather(routes, ("core", "z", "y"), axis=0, tiled=False)
        named = named.reshape((2, z_count, y_count) + routes.shape)
        named = jnp.any(named == expert_at, axis=-1)
        named = jnp.where(core == 0, named, named[::-1])
        named = jnp.take(jnp.take(named, z_from, axis=1), y_from, axis=2)
        named = named.transpose(0, 3, 1, 2, 4).reshape(2 * micro_count, seq_len)
        earlier = jnp.arange(seq_len)[:, None] < jnp.arange(seq_len)[None, :]
        rank = mm(named.astype(BF16), earlier.astype(BF16)).astype(jnp.int32)
        rank = jnp.where(named, rank, -1)
        select = rank[:, None, :] == jnp.arange(slots, dtype=jnp.int32)[None, :, None]
        select = select.reshape(2, micro_count, slots, seq_len)
        select_low = select.astype(BF16)

        state = []
        for m in range(micro_count):
            own = tokens[m]
            rows = gather(own).astype(F32)
            row_scale = norm_scale(rows)
            normed = (rows * row_scale * gain_attn).astype(BF16)
            raw = mm(normed, qkv)
            query_raw, key_raw = raw[:, :local_width], raw[:, local_width : 2 * local_width]
            value = raw[:, 2 * local_width :].astype(BF16)
            squares = jnp.stack(
                [jnp.sum(query_raw * query_raw, axis=1), jnp.sum(key_raw * key_raw, axis=1)]
            )
            squares = sum_ep(squares, z_count, y_count)
            scales = lax.rsqrt(squares / width + NORM_EPSILON)
            query_scale, key_scale = scales[0][:, None], scales[1][:, None]
            query = rope(query_raw * query_scale * gain_query).astype(BF16)
            key = rope(key_raw * key_scale * gain_key).astype(BF16)
            probs, attended = [], []
            for h in range(heads_here):
                at = slice(h * head_dim, (h + 1) * head_dim)
                scores = mm_cols(query[:, at], key[:, at]) * score_scale
                scores = jnp.where(allowed, scores, -1e30)
                scores = jnp.exp(scores - jnp.max(scores, axis=-1, keepdims=True))
                prob = scores / jnp.sum(scores, axis=-1, keepdims=True)
                probs.append(prob)
                attended.append(mm(prob.astype(BF16), value[:, at]).astype(BF16))
            attended = jnp.concatenate(attended, axis=1)
            resid_mid = own.astype(F32) + scatter(mm(attended, out_here))
            state.append(
                dict(
                    own=own,
                    rows=rows,
                    row_scale=row_scale,
                    normed=normed,
                    query_raw=query_raw,
                    key_raw=key_raw,
                    query_scale=query_scale,
                    key_scale=key_scale,
                    query=query,
                    key=key,
                    value=value,
                    probs=probs,
                    attended=attended,
                    resid_mid=resid_mid,
                )
            )

        router_grad = jnp.zeros((width, expert_count), F32)
        outputs = []
        moe_rows, act_rows, pair_rows, gate_rows, up_rows = [], [], [], [], []
        for m in range(micro_count):
            st = state[m]
            moe_scale = norm_scale(st["resid_mid"])
            st["moe_scale"] = moe_scale
            moe_own = (st["resid_mid"] * moe_scale * gain_moe).astype(BF16)
            moe_all = [gather(moe_own)]
            moe_all.append(lax.ppermute(moe_all[0], "core", SWAP))
            cot_all = [gather(cotangent[m])]
            cot_all.append(lax.ppermute(cot_all[0], "core", SWAP))
            incoming = jnp.concatenate(
                [mm(select_low[i, m], moe_all[i]).astype(BF16) for i in range(2)], axis=0
            )
            grads_in = jnp.concatenate(
                [mm(select_low[i, m], cot_all[i]).astype(BF16) for i in range(2)], axis=0
            )
            router_probs = [
                jax.nn.softmax(mm(moe_all[i], full_router), axis=-1) for i in range(2)
            ]
            mine = [jnp.sum(jnp.where(expert_hot, p, 0.0), axis=-1) for p in router_probs]
            weights = jnp.concatenate(
                [
                    jnp.sum(jnp.where(select[i, m], mine[i][None, :], 0.0), axis=-1)
                    for i in range(2)
                ]
            )[:, None]
            gate_pre = mm(incoming, gate_w)
            up_pre = mm(incoming, up_w)
            sigmoid = jax.nn.sigmoid(gate_pre)
            activation = (gate_pre * sigmoid * up_pre).astype(BF16)
            expert_rows = mm(activation, down_w)
            wide_grads = grads_in.astype(F32)
            gate_grads = jnp.sum(wide_grads * expert_rows, axis=-1)
            pair_grad = (weights * wide_grads).astype(BF16)
            grad_act = mm_cols(pair_grad, down_w)
            grad_up = (grad_act * gate_pre * sigmoid).astype(BF16)
            grad_gate = (
                grad_act * up_pre * sigmoid * (1.0 + gate_pre * (1.0 - sigmoid))
            ).astype(BF16)
            row_grad = (mm_cols(grad_gate, gate_w) + mm_cols(grad_up, up_w)).astype(BF16)
            weighted = (weights * expert_rows).astype(BF16)
            moe_rows.append(incoming)
            act_rows.append(activation)
            pair_rows.append(pair_grad)
            gate_rows.append(grad_gate)
            up_rows.append(grad_up)
            grad_parts, out_parts = [], []
            for i in range(2):
                at = slice(i * slots, (i + 1) * slots)
                token_grads = jnp.sum(
                    jnp.where(select[i, m], gate_grads[at][:, None], 0.0), axis=0
                )
                through = (token_grads * mine[i])[:, None]
                logits_grad = jnp.where(expert_hot, through, 0.0) - router_probs[i] * through
                logits_grad = logits_grad.astype(BF16)
                router_grad = router_grad + mm_rows(moe_all[i], logits_grad)
                grad_parts.append(
                    mm_rows(select_low[i, m], row_grad[at]) + mm_cols(logits_grad, full_router)
                )
                out_parts.append(mm_rows(select_low[i, m], weighted[at]))
            grad_part = grad_parts[0] + lax.ppermute(
                grad_parts[1].astype(BF16), "core", SWAP
            ).astype(F32)
            st["grad_moe_in"] = scatter(grad_part)
            out_part = out_parts[0] + lax.ppermute(
                out_parts[1].astype(BF16), "core", SWAP
            ).astype(F32)
            outputs.append(out_part)

        moe_cat = jnp.concatenate(moe_rows, axis=0)

        def over_x(part):
            low = part.astype(BF16)
            parts = [low] + [lax.ppermute(low, "x", turn(x_count, i)) for i in range(1, x_count)]
            if x_count > 2:
                parts = unturn(parts, x_at)
            total = parts[0].astype(F32)
            for item in parts[1:]:
                total = total + item.astype(F32)
            return total.astype(BF16)

        def both_cores(own, axis):
            other = lax.ppermute(own, "core", SWAP)
            first, second = jnp.where(core == 0, own, other), jnp.where(core == 0, other, own)
            if local_experts == 2:
                return jnp.stack([first, second]).astype(F32)
            return jnp.concatenate([first, second], axis=axis)[None].astype(F32)

        d_down = both_cores(
            over_x(mm_rows(jnp.concatenate(act_rows, axis=0), jnp.concatenate(pair_rows, axis=0))),
            0,
        )
        d_gate = both_cores(over_x(mm_rows(moe_cat, jnp.concatenate(gate_rows, axis=0))), 1)
        d_up = both_cores(over_x(mm_rows(moe_cat, jnp.concatenate(up_rows, axis=0))), 1)

        d_tokens, block_out = [], []
        moe_gain_grad = jnp.zeros((width,), F32)
        attn_gain_grad = jnp.zeros((width,), F32)
        query_gain_grad = jnp.zeros((local_width,), F32)
        key_gain_grad = jnp.zeros((local_width,), F32)
        out_grads, attended_all, raw_grads, normed_all = [], [], [], []
        for m in range(micro_count):
            st = state[m]
            resid_mid, scale = st["resid_mid"], st["moe_scale"]
            grad = st["grad_moe_in"]
            moe_gain_grad = moe_gain_grad + jnp.sum(grad * resid_mid * scale, axis=0)
            inner = grad * gain_moe
            grad_mid = (
                cotangent[m].astype(F32)
                + scale * inner
                - resid_mid * (scale**3 * jnp.mean(resid_mid * inner, axis=-1, keepdims=True))
            )
            grad_attn = gather(grad_mid.astype(BF16))
            out_grads.append(grad_attn)
            attended_all.append(st["attended"])
            grad_attended = mm_cols(grad_attn, out_here).astype(BF16)
            query, key, value = st["query"], st["key"], st["value"]
            grad_query, grad_key, grad_value = [], [], []
            for h in range(heads_here):
                at = slice(h * head_dim, (h + 1) * head_dim)
                prob = st["probs"][h]
                grad_value.append(mm_rows(prob.astype(BF16), grad_attended[:, at]).astype(BF16))
                grad_pa = mm_cols(grad_attended[:, at], value[:, at])
                delta = jnp.sum(prob * grad_pa, axis=-1, keepdims=True)
                grad_scores = (prob * (grad_pa - delta)).astype(BF16)
                grad_query.append(mm(grad_scores, key[:, at]) * score_scale)
                grad_key.append(mm_rows(grad_scores, query[:, at]) * score_scale)
            grad_query = rope_back(jnp.concatenate(grad_query, axis=1))
            grad_key = rope_back(jnp.concatenate(grad_key, axis=1))
            inner_query, inner_key = grad_query * gain_query, grad_key * gain_key
            query_raw, key_raw = st["query_raw"], st["key_raw"]
            query_scale, key_scale = st["query_scale"], st["key_scale"]
            query_gain_grad = query_gain_grad + jnp.sum(grad_query * query_raw * query_scale, axis=0)
            key_gain_grad = key_gain_grad + jnp.sum(grad_key * key_raw * key_scale, axis=0)
            means = jnp.stack(
                [jnp.sum(inner_query * query_raw, axis=1), jnp.sum(inner_key * key_raw, axis=1)]
            )
            means = sum_ep(means, z_count, y_count) / width
            query_back = (
                query_scale * inner_query - query_raw * (query_scale**3 * means[0][:, None])
            ).astype(BF16)
            key_back = (
                key_scale * inner_key - key_raw * (key_scale**3 * means[1][:, None])
            ).astype(BF16)
            raw_grad = jnp.concatenate([query_back, key_back] + grad_value, axis=1)
            raw_grads.append(raw_grad)
            normed_all.append(st["normed"])
            normed_part = mm_cols(raw_grad, qkv)
            attn_gain_grad = attn_gain_grad + jnp.sum(
                normed_part * st["rows"] * st["row_scale"], axis=0
            )
            grad_normed = scatter(normed_part)
            resid_in = st["own"].astype(F32)
            in_scale = norm_scale(resid_in)
            inner = grad_normed * gain_attn
            d_tokens.append(
                grad_mid
                + in_scale * inner
                - resid_in * (in_scale**3 * jnp.mean(resid_in * inner, axis=-1, keepdims=True))
            )
            block_out.append((resid_mid + scatter(outputs[m])).astype(BF16))

        qkv_grad = mm_rows(jnp.concatenate(normed_all, axis=0), jnp.concatenate(raw_grads, axis=0))
        qkv_grad = scatter_grp(qkv_grad.reshape(grp_size, -1, 3 * local_width), x_count)
        qkv_grad = qkv_grad.astype(BF16).reshape(group_size, weight_rows, 3 * local_width)
        qkv_grad = lax.all_to_all(
            qkv_grad, ("z", "y"), split_axis=0, concat_axis=0, tiled=True
        ).astype(F32)

        def by_row(grads):
            shaped = grads.reshape(head_sets, pieces, weight_rows, heads_here, head_dim)
            return shaped.transpose(2, 1, 3, 0, 4).reshape(weight_rows, width)

        d_query = by_row(qkv_grad[:, :, :local_width])
        d_key = by_row(qkv_grad[:, :, local_width : 2 * local_width])
        d_value = by_row(qkv_grad[:, :, 2 * local_width :])
        out_grad = mm_rows(
            jnp.concatenate(attended_all, axis=0), jnp.concatenate(out_grads, axis=0)
        )
        out_grad = scatter_grp(out_grad.reshape(grp_size, weight_rows, width), x_count)
        d_out = lax.ppermute(
            out_grad.astype(BF16), ALL, [(user, home) for home, user in out_pairs]
        ).astype(F32)

        device_count = grp_size * group_size
        vectors = jnp.stack(
            [
                attn_gain_grad,
                head_part_back(query_gain_grad),
                head_part_back(key_gain_grad),
                moe_gain_grad,
            ]
        )
        vectors = vectors.reshape(4, device_count, weight_rows).transpose(1, 0, 2)
        small_grads = jnp.concatenate(
            [
                vectors.reshape(device_count, 4 * weight_rows),
                router_grad.reshape(device_count, weight_rows * expert_count),
            ],
            axis=1,
        )
        small_grads = lax.all_to_all(small_grads, ALL, split_axis=0, concat_axis=0, tiled=True)
        small_grads = jnp.sum(small_grads, axis=0)
        gain_grads = small_grads[: 4 * weight_rows].reshape(4, weight_rows)
        d_router = small_grads[4 * weight_rows :].reshape(weight_rows, expert_count)

        shape = (micro_count, seq_parts, row_count, width)
        return (
            jnp.stack(block_out).reshape(shape),
            jnp.stack(d_tokens).reshape(shape),
            gain_grads[0],
            d_query,
            d_key,
            d_value,
            gain_grads[1],
            gain_grads[2],
            d_out,
            gain_grads[3],
            d_router,
            d_gate,
            d_up,
            d_down,
        )

    return per_device


def solution(mesh):
    devices = mesh.devices
    x_count, y_count, z_count = (
        len({device.coords[axis] for device in devices.flat}) for axis in range(3)
    )
    fine = Mesh(devices.reshape(x_count, 2, z_count, y_count), ALL)
    grp, ep = ("x", "core"), ("z", "y")
    by_token = P(None, grp, ep, None)
    vector, matrix, expert = P(ALL), P(ALL, None), P(ep, None, None)
    return jax.shard_map(
        make_per_device(x_count, z_count, y_count),
        mesh=fine,
        in_specs=(
            by_token,
            by_token,
            vector,
            matrix,
            matrix,
            matrix,
            vector,
            vector,
            matrix,
            vector,
            matrix,
            expert,
            expert,
            expert,
            by_token,
        ),
        out_specs=(
            by_token,
            by_token,
            vector,
            matrix,
            matrix,
            matrix,
            vector,
            vector,
            matrix,
            vector,
            matrix,
            expert,
            expert,
            expert,
        ),
        check_vma=False,
    )
```

```python
import functools
import math

import jax
import jax.numpy as jnp
from jax import lax
from jax.experimental import pallas as pl
from jax.experimental.pallas import tpu as pltpu
from jax.sharding import Mesh, PartitionSpec as P

HEADS = 16
CAP = 36
NORM_EPSILON = 1e-05
ROPE_BASE = 10000.0
ALL = ("x", "core", "z", "y")
SWAP = ((0, 1), (1, 0))
F32 = jnp.float32
BF16 = jnp.bfloat16


def turn(count, step):
    return tuple((i, (i + step) % count) for i in range(count))


def flip(count, bits):
    return tuple((i, i ^ bits) for i in range(count))


def after(values, *others):
    return lax.optimization_barrier((values,) + others)[0]


def mm(left, right):
    return jnp.dot(left, right, preferred_element_type=F32)


def mm_rows(left, right):
    return lax.dot_general(left, right, (((0,), (0,)), ((), ())), preferred_element_type=F32)


def mm_cols(left, right):
    return lax.dot_general(left, right, (((1,), (1,)), ((), ())), preferred_element_type=F32)


def unturn(items, index):
    count = len(items)
    if count == 1:
        return items
    placed = []
    for place in range(count):
        chosen = items[(0 - place) % count]
        for at in range(1, count):
            chosen = jnp.where(index == at, items[(at - place) % count], chosen)
        placed.append(chosen)
    return placed


def gather_ep(block, y_count, micro_count):
    by_z = {0: block}
    by_z[2] = lax.ppermute(block, "z", flip(4, 2))
    by_z[1] = lax.ppermute(block, "z", flip(4, 1))
    blocks = {}

    def along_y(a):
        blocks[a, 0] = by_z[a]
        for j in range(1, y_count):
            blocks[a, j] = lax.ppermute(by_z[a], "y", flip(y_count, j))

    along_y(0)
    by_z[3] = lax.ppermute(by_z[2], "z", flip(4, 1))
    for a in (1, 2, 3):
        along_y(a)
    rows = block.shape[0] // micro_count
    return jnp.concatenate(
        [
            blocks[a, j][m * rows : (m + 1) * rows]
            for m in range(micro_count)
            for a in range(4)
            for j in range(y_count)
        ],
        axis=0,
    )


def scatter_ep(part, y_count, micro_count):
    rows = part.shape[0] // (4 * y_count * micro_count)

    def piece(a, j):
        starts = [((m * 4 + a) * y_count + j) * rows for m in range(micro_count)]
        return jnp.concatenate([part[at : at + rows] for at in starts], axis=0)

    sums = {}

    def along_y(a):
        total = piece(a, 0).astype(F32)
        for j in range(1, y_count):
            arrived = lax.ppermute(piece(a, j).astype(BF16), "y", flip(y_count, j))
            total = total + arrived.astype(F32)
        sums[a] = total

    along_y(3)
    along_y(2)
    sums[2] = sums[2] + lax.ppermute(sums[3].astype(BF16), "z", flip(4, 1)).astype(F32)
    across = lax.ppermute(sums[2].astype(BF16), "z", flip(4, 2)).astype(F32)
    along_y(1)
    near = lax.ppermute(sums[1].astype(BF16), "z", flip(4, 1)).astype(F32)
    along_y(0)
    return sums[0] + near + across


def sum_ep(values, y_count, micro_count):
    shape = values.shape
    values = values.reshape(shape[0] * micro_count, 4, y_count, -1)

    def moved(source, axis, count, at, bits):
        arrived = lax.ppermute(source, axis, flip(count, bits))
        picked = [lax.index_in_dim(arrived, b ^ bits, at, keepdims=True) for b in range(count)]
        return jnp.concatenate(picked, axis=at)

    along = values
    for j in range(1, y_count):
        along = along + moved(values, "y", y_count, 2, j)
    total = along
    for a in (1, 2, 3):
        total = total + moved(along, "z", 4, 1, a)
    return total.reshape(shape)


def gather_grp(block, x_count):
    x_at, core = lax.axis_index("x"), lax.axis_index("core")
    mine = [block] + [lax.ppermute(block, "x", turn(x_count, i)) for i in range(1, x_count)]
    theirs = [lax.ppermute(item, "core", SWAP) for item in mine]
    mine, theirs = unturn(mine, x_at), unturn(theirs, x_at)
    stacked = []
    for own, other in zip(mine, theirs):
        stacked += [jnp.where(core == 0, own, other), jnp.where(core == 0, other, own)]
    return jnp.stack(stacked)


def keep_core(parts, x_count):
    core = lax.axis_index("core")
    parts = parts.reshape((x_count, 2) + parts.shape[1:])
    away = lax.dynamic_index_in_dim(parts, 1 - core, 1, keepdims=False).astype(BF16)
    kept = lax.dynamic_index_in_dim(parts, core, 1, keepdims=False)
    return kept + lax.ppermute(away, "core", SWAP).astype(F32)


def keep_x(kept, x_count):
    x_at = lax.axis_index("x")
    total = lax.dynamic_index_in_dim(kept, x_at, 0, keepdims=False)
    for i in range(1, x_count):
        away = lax.dynamic_index_in_dim(kept, (x_at - i) % x_count, 0, keepdims=False)
        total = total + lax.ppermute(away.astype(BF16), "x", turn(x_count, -i)).astype(F32)
    return total


def experts_kernel(count, which, hot_ref, router_ref, *refs):
    select, select_t, moe, cot = (refs[i * count : (i + 1) * count] for i in range(4))
    gate_ref, up_ref, down_ref = refs[4 * count : 4 * count + 3]
    rest = refs[4 * count + 3 :]
    grad_out, row_out = rest[:count], rest[count : 2 * count]
    rows_ref, cot_ref, act_ref, dgate_ref, dup_ref, logit_ref = rest[2 * count : 2 * count + 6]
    total_ref, back_ref, prob_ref, weight_ref, share_ref = rest[2 * count + 6 :]
    step = pl.program_id(0)
    slots = select[0].shape[1]

    @pl.when(step == 0)
    def _():
        for i in range(count):
            at = pl.ds(i * slots, slots)
            rows_ref[at, :] = mm(select[i][0], moe[i][...]).astype(BF16)
            cot_ref[at, :] = mm(select[i][0], cot[i][...]).astype(BF16)
        logits = mm(rows_ref[...], router_ref[...])
        lane = lax.broadcasted_iota(jnp.int32, logits.shape, 1)
        logits = jnp.where(lane < which, logits, -1e30)
        logits = jnp.exp(logits - jnp.max(logits, axis=1, keepdims=True))
        prob = logits / jnp.sum(logits, axis=1, keepdims=True)
        prob_ref[...] = prob
        weight = jnp.sum(prob * hot_ref[...], axis=1, keepdims=True)
        weight_ref[...] = jnp.broadcast_to(weight, weight_ref.shape)
        share_ref[...] = jnp.zeros_like(share_ref)

    weight = weight_ref[:, :1]
    gate_w, up_w, down_w = gate_ref[0], up_ref[0], down_ref[0]
    gate = mm(rows_ref[...], gate_w)
    up = mm(rows_ref[...], up_w)
    sigmoid = jax.nn.sigmoid(gate)
    silu = gate * sigmoid
    active = silu * up
    act = (weight * active).astype(BF16)
    act_ref[...] = act
    grad = mm_cols(cot_ref[...], down_w)
    share_ref[...] += jnp.broadcast_to(
        jnp.sum(active * grad, axis=1, keepdims=True), share_ref.shape
    )
    grad = weight * grad
    dup = (grad * silu).astype(BF16)
    dgate = (grad * up * (sigmoid + silu * (1.0 - sigmoid))).astype(BF16)
    dup_ref[...] = dup
    dgate_ref[...] = dgate
    weighted = mm(act, down_w)
    back = mm_cols(dgate, gate_w) + mm_cols(dup, up_w)

    @pl.when(step == 0)
    def _():
        total_ref[...] = weighted
        back_ref[...] = back

    @pl.when(step > 0)
    def _():
        total_ref[...] += weighted
        back_ref[...] += back

    @pl.when(step == pl.num_programs(0) - 1)
    def _():
        logit = (share_ref[...] * weight_ref[...] * (hot_ref[...] - prob_ref[...])).astype(BF16)
        logit_ref[...] = logit
        for i in range(count):
            at = pl.ds(i * slots, slots)
            back = (back_ref[at, :] + mm_cols(logit_ref[at, :], router_ref[...])).astype(BF16)
            grad_out[i][...] = mm(select_t[i][0], back).astype(BF16)
            row_out[i][...] = mm(select_t[i][0], total_ref[at, :].astype(BF16)).astype(BF16)


def run_experts(
    sets, at, hot, router, select, select_t, micro, moe, cot, w_gate, w_up, w_down, experts, hidden
):
    count, (slots, seq_len), width = len(sets), select.shape[1:], router.shape[0]
    block = 256
    steps, rows = hidden // block, count * slots

    def whole(array):
        return pl.BlockSpec(
            array.shape, lambda f, at: (0,) * array.ndim, pipeline_mode=pl.Buffered(1)
        )

    def kept(shape):
        return pl.BlockSpec(shape, lambda f, at: (0, 0))

    wide = pl.BlockSpec((1, width, block), lambda f, at: (at[0], 0, at[1] + f))
    tall = pl.BlockSpec((1, block, width), lambda f, at: (at[0], at[1] + f, 0))
    hidden_rows = pl.BlockSpec((rows, block), lambda f, at: (0, f))
    one_micro = pl.BlockSpec(
        (seq_len, width), lambda f, at: (micro, 0), pipeline_mode=pl.Buffered(1)
    )
    tables = [array for array in (select, select_t) for _ in sets]
    table_specs = [
        pl.BlockSpec(
            (1,) + array.shape[1:],
            functools.partial(lambda one, f, at: (one, 0, 0), one),
            pipeline_mode=pl.Buffered(1),
        )
        for array in (select, select_t)
        for one in sets
    ]
    one_micro = pl.BlockSpec(
        (seq_len, width), lambda f, at: (micro, 0), pipeline_mode=pl.Buffered(1)
    )
    tables = [array for array in (select, select_t) for _ in sets]
    table_specs = [
        pl.BlockSpec(
            (1,) + array.shape[1:],
            functools.partial(lambda one, f, at: (one, 0, 0), one),
            pipeline_mode=pl.Buffered(1),
        )
        for array in (select, select_t)
        for one in sets
    ]
    tokens = jax.ShapeDtypeStruct((seq_len, width), BF16)
    gathered = jax.ShapeDtypeStruct((rows, width), BF16)
    inner = jax.ShapeDtypeStruct((rows, hidden), BF16)
    result = pl.pallas_call(
        lambda at, *refs: experts_kernel(count, experts, *refs),
        grid_spec=pltpu.PrefetchScalarGridSpec(
            num_scalar_prefetch=1,
            grid=(steps,),
            in_specs=[whole(hot), whole(router)]
            + table_specs
            + [one_micro] * (2 * count)
            + [wide, wide, tall],
            out_specs=[kept((seq_len, width))] * (2 * count)
            + [kept((rows, width))] * 2
            + [hidden_rows] * 3
            + [kept((rows, 128))],
            scratch_shapes=[pltpu.VMEM((rows, width), F32)] * 2
            + [pltpu.VMEM((rows, 128), F32)] * 3,
        ),
        out_shape=[tokens] * (2 * count)
        + [gathered] * 2
        + [inner] * 3
        + [jax.ShapeDtypeStruct((rows, 128), BF16)],
        compiler_params=pltpu.CompilerParams(
            dimension_semantics=("arbitrary",), vmem_limit_bytes=60 * 2**20
        ),
        cost_estimate=pl.CostEstimate(
            flops=12 * rows * hidden * width + 8 * rows * seq_len * width,
            bytes_accessed=6 * hidden * width + 16 * seq_len * width + 8 * rows * width,
            transcendentals=rows * hidden,
        ),
        name="experts",
    )(at, hot, router, *tables, *moe, *cot, w_gate, w_up, w_down)
    return result[:count], result[count : 2 * count], result[2 * count :]


def norm_scale(values):
    return lax.rsqrt(jnp.mean(values * values, axis=-1, keepdims=True) + NORM_EPSILON)


def make_per_device(x_count, z_count, y_count):
    group_size = z_count * y_count
    grp_size = 2 * x_count

    assert z_count == 4

    def per_device(
        tokens,
        routes,
        attn_gain,
        w_query,
        w_key,
        w_value,
        query_gain,
        key_gain,
        w_out,
        moe_gain,
        w_router,
        w_gate,
        w_up,
        w_down,
        cotangent,
    ):
        micro_count, seq_parts, row_count, width = tokens.shape
        top_count = routes.shape[3]
        tokens = tokens.reshape(micro_count, row_count, width)
        routes = routes.reshape(micro_count, row_count, top_count)
        cotangent = cotangent.reshape(micro_count, row_count, width)
        expert_count = w_router.shape[1]
        seq_len = row_count * group_size
        head_dim = width // HEADS
        half = head_dim // 2
        score_scale = 1.0 / math.sqrt(head_dim)
        weight_rows = w_query.shape[0]
        pieces = head_dim // weight_rows
        heads_here = grp_size // pieces
        head_sets = group_size // pieces
        local_width = heads_here * head_dim
        x_at, core = lax.axis_index("x"), lax.axis_index("core")
        z_at, y_at = lax.axis_index("z"), lax.axis_index("y")
        ep_at = z_at * y_count + y_at
        set_at, piece_at = ep_at // pieces, ep_at % pieces
        slots = CAP * group_size
        local_experts = w_gate.shape[0]
        ff_width = w_gate.shape[2]

        def gather(block):
            return gather_ep(block.reshape(-1, width), y_count, micro_count)

        def scatter(part):
            return scatter_ep(part, y_count, micro_count)

        def by_owner(weight):
            shaped = weight.reshape(weight_rows, pieces, heads_here, head_sets, head_dim)
            return shaped.transpose(3, 1, 0, 2, 4).reshape(group_size, weight_rows, local_width)

        qkv = jnp.concatenate([by_owner(w) for w in (w_query, w_key, w_value)], axis=2)
        qkv = lax.all_to_all(qkv, ("z", "y"), split_axis=0, concat_axis=0, tiled=True)
        small = jnp.concatenate(
            [w_router]
            + [g[:, None] for g in (attn_gain, query_gain, key_gain, moe_gain)],
            axis=1,
        ).reshape(-1)
        naming = jnp.any(
            routes.reshape(1, -1, top_count)
            == jnp.arange(expert_count, dtype=jnp.int32)[:, None, None],
            axis=-1,
        ).astype(BF16)
        if local_experts == 2:
            naming = naming.reshape(group_size, 2, -1).transpose(1, 0, 2)
        else:
            assert local_experts == 1
            naming = jnp.broadcast_to(naming[None], (2,) + naming.shape)
        device_count = grp_size * group_size
        naming = jnp.broadcast_to(naming[None], (x_count,) + naming.shape).reshape(device_count, -1)
        small = jnp.concatenate(
            [jnp.broadcast_to(small[None], (device_count, small.shape[0])), naming], axis=1
        )
        small = lax.all_to_all(after(small, qkv), ALL, split_axis=0, concat_axis=0, tiled=True)
        named = small[:, -micro_count * row_count :]
        small = small[:, : -micro_count * row_count].reshape(width, expert_count + 4)
        full_router = small[:, :expert_count]
        gains = small[:, expert_count:].astype(F32).T
        gain_attn, gain_query, gain_key, gain_moe = gains[0:1], gains[1], gains[2], gains[3:4]

        def head_part(vector):
            shaped = vector.reshape(pieces, heads_here, head_sets, head_dim)
            shaped = lax.dynamic_index_in_dim(shaped, piece_at, 0, keepdims=False)
            return lax.dynamic_index_in_dim(shaped, set_at, 1, keepdims=False).reshape(1, -1)

        def head_part_back(vector):
            piece_hot = jnp.arange(pieces) == piece_at
            set_hot = jnp.arange(head_sets) == set_at
            hot = piece_hot[:, None, None, None] & set_hot[None, None, :, None]
            return jnp.where(hot, vector.reshape(1, heads_here, 1, head_dim), 0.0).reshape(-1)

        gain_query, gain_key = head_part(gain_query), head_part(gain_key)

        sent_qkv = qkv
        qkv = gather_grp(qkv.reshape(group_size * weight_rows, 3 * local_width), x_count)
        qkv = qkv.reshape(width, 3 * local_width)
        out_pairs = []
        for s in range(head_sets):
            for t in range(pieces):
                for h in range(heads_here):
                    for p in range(pieces):
                        home = (t * heads_here + h) * group_size + s * pieces + p
                        user = (h * pieces + p) * group_size + s * pieces + t
                        out_pairs.append((home, user))
        out_here = lax.ppermute(w_out, ALL, out_pairs)
        out_here = gather_grp(out_here, x_count).reshape(local_width, width)

        z_from = z_at ^ jnp.arange(z_count, dtype=jnp.int32)
        y_from = y_at ^ jnp.arange(y_count, dtype=jnp.int32)
        block_from = z_from[:, None] * y_count + y_from[None, :]
        positions = (
            block_from.reshape(-1)[:, None] * row_count
            + jnp.arange(row_count, dtype=jnp.int32)[None, :]
        ).reshape(-1)
        frequency = jnp.exp(
            -math.log(ROPE_BASE) * jnp.arange(half, dtype=F32) * 2.0 / head_dim
        )
        angles = positions.astype(F32)[:, None] * frequency[None, :]
        cosine, sine = jnp.cos(angles), jnp.sin(angles)
        cos_both = jnp.concatenate([cosine, cosine], axis=1)
        sin_both = jnp.concatenate([-sine, sine], axis=1)
        allowed = positions[:, None] >= positions[None, :]

        def halves_swapped(values):
            parts = []
            for h in range(heads_here):
                at = h * head_dim
                parts += [values[:, at + half : at + head_dim], values[:, at : at + half]]
            return jnp.concatenate(parts, axis=1)

        wide_cos = jnp.tile(cos_both, (micro_count, heads_here))
        wide_sin = jnp.tile(sin_both, (micro_count, heads_here))

        def rope(values):
            return values * wide_cos + halves_swapped(values) * wide_sin

        def rope_back(values):
            return values * wide_cos - halves_swapped(values) * wide_sin

        if local_experts == 2:
            expert_at, hidden = ep_at * 2 + core, ff_width
            expert_place = jnp.stack([core, 0 * core]).astype(jnp.int32)
        else:
            expert_at, hidden = ep_at, ff_width // 2
            expert_place = jnp.stack([0 * core, core * (hidden // 256)]).astype(jnp.int32)
        hot = (jnp.arange(128, dtype=jnp.int32) == expert_at).astype(F32)[None]
        padded_router = jnp.pad(full_router, ((0, 0), (0, 128 - expert_count)))

        named = named.reshape((x_count, 2, z_count, y_count, micro_count, row_count))
        named = lax.dynamic_index_in_dim(named, x_at, 0, keepdims=False)
        named = jnp.where(core == 0, named, named[::-1])
        named = jnp.take(jnp.take(named, z_from, axis=1), y_from, axis=2)
        named = named.transpose(3, 0, 1, 2, 4).reshape(2 * micro_count, seq_len) > 0.5
        earlier = jnp.arange(seq_len)[:, None] < jnp.arange(seq_len)[None, :]
        rank = mm(named.astype(BF16), earlier.astype(BF16)).astype(jnp.int32)
        rank = jnp.where(named, rank, -1)
        slot_ids = jnp.arange(slots, dtype=jnp.int32)
        select = (rank[:, None, :] == slot_ids[None, :, None]).astype(BF16)
        select_t = (rank[:, :, None] == slot_ids[None, None, :]).astype(BF16)

        def micro_rows(m):
            return slice(m * seq_len, (m + 1) * seq_len)

        def head_cols(h):
            return slice(h * head_dim, (h + 1) * head_dim)

        own = tokens.reshape(-1, width).astype(F32)
        micros = range(micro_count)
        rows = gather(tokens)
        low_rows = rows
        rows = rows.astype(F32)
        row_scale = norm_scale(rows)
        normed = (rows * row_scale * gain_attn).astype(BF16)
        raw = mm(normed, qkv)
        query_raw, key_raw = raw[:, :local_width], raw[:, local_width : 2 * local_width]
        value = raw[:, 2 * local_width :].astype(BF16)
        squares = jnp.stack(
            [jnp.sum(query_raw * query_raw, axis=1), jnp.sum(key_raw * key_raw, axis=1)]
        )
        squares = sum_ep(squares, y_count, micro_count)
        cot_all = [gather(after(cotangent, low_rows))]
        scales = lax.rsqrt(squares / width + NORM_EPSILON)
        query_scale, key_scale = scales[0][:, None], scales[1][:, None]
        query = rope(query_raw * query_scale * gain_query).astype(BF16)
        key = rope(key_raw * key_scale * gain_key).astype(BF16)
        probs, attended = {}, []
        for m in range(micro_count):
            here = []
            for h in range(heads_here):
                at = micro_rows(m), head_cols(h)
                scores = mm_cols(query[at], key[at]) * score_scale
                scores = jnp.where(allowed, scores, -1e30)
                scores = jnp.exp(scores - jnp.max(scores, axis=-1, keepdims=True))
                prob = scores / jnp.sum(scores, axis=-1, keepdims=True)
                probs[m, h] = prob
                here.append(mm(prob.astype(BF16), value[at]).astype(BF16))
            attended.append(jnp.concatenate(here, axis=1))
        attended = jnp.concatenate(attended, axis=0)
        resid_mid = own + scatter(mm(attended, out_here).astype(BF16))

        def with_other_core(parts):
            arrived = [lax.ppermute(p[1], "core", SWAP) for p in parts]
            return jnp.concatenate(
                [
                    (p[0].astype(F32) + other.astype(F32)).astype(BF16)
                    for p, other in zip(parts, arrived)
                ],
                axis=0,
            )

        moe_scale = norm_scale(resid_mid)
        moe_all = [gather((resid_mid * moe_scale * gain_moe).astype(BF16))]
        moe_all.append(lax.ppermute(moe_all[0], "core", SWAP))
        cot_all.append(lax.ppermute(cot_all[0], "core", SWAP))
        saved, out_parts, grad_parts = [], [], []
        for m in micros:
            sets = [slice(0, 2)] if slots <= 288 else [slice(0, 1), slice(1, 2)]
            grads, outs = [], []
            for here in sets:
                grad, out, rest = run_experts(
                    range(2 * m, 2 * m + 2)[here],
                    expert_place,
                    hot,
                    padded_router,
                    select,
                    select_t,
                    m,
                    moe_all[here],
                    cot_all[here],
                    w_gate,
                    w_up,
                    w_down,
                    expert_count,
                    hidden,
                )
                grads, outs = grads + list(grad), outs + list(out)
                saved.append(rest)
            grad_parts.append(grads)
            out_parts.append(outs)
        grad_sum = with_other_core(grad_parts)
        grad_moe_in = scatter(grad_sum)

        def over_pairs(left, right):
            total = None
            for rest in saved:
                term = mm_rows(rest[left], rest[right])
                total = term if total is None else total + term
            return total

        def halves(part):
            middle = part.shape[0] // 2
            return [part[:middle], part[middle:]]

        def over_x(low, start=None):
            sent = low if start is None else after(low, start)
            return [low] + [
                lax.ppermute(sent, "x", turn(x_count, i)) for i in range(1, x_count)
            ]

        def summed(parts, start):
            parts = [parts[0]] + [after(p, start) for p in parts[1:]]
            if x_count > 2:
                parts = unturn(parts, x_at)
            total = parts[0].astype(F32)
            for item in parts[1:]:
                total = total + item.astype(F32)
            return total.astype(BF16)

        def both_cores(sums, axis):
            first, second = [], []
            for own_part in sums:
                other = lax.ppermute(own_part, "core", SWAP)
                first.append(jnp.where(core == 0, own_part, other))
                second.append(jnp.where(core == 0, other, own_part))
            first, second = jnp.concatenate(first), jnp.concatenate(second)
            if local_experts == 2:
                return jnp.stack([first, second]).astype(F32)
            return jnp.concatenate([first, second], axis=axis)[None].astype(F32)

        down_low = over_pairs(2, 1).astype(BF16)
        saved = [[after(r, grad_sum) for r in rest] for rest in saved]
        gate_low = over_pairs(0, 3).astype(BF16)
        up_low = over_pairs(0, 4).astype(BF16)
        router_grad = over_pairs(0, 5)[:, :expert_count]
        down_parts = [over_x(p) for p in halves(down_low)]
        gate_parts = [over_x(p) for p in halves(gate_low)]
        up_first, up_second = halves(up_low)

        grad_out = cotangent.reshape(-1, width).astype(F32)
        moe_gain_grad = jnp.sum(grad_moe_in * resid_mid * moe_scale, axis=0)
        inner = grad_moe_in * gain_moe
        grad_mid = (
            grad_out
            + moe_scale * inner
            - resid_mid * (moe_scale**3 * jnp.mean(resid_mid * inner, axis=-1, keepdims=True))
        )
        grad_attn = gather(grad_mid.astype(BF16))
        mixture = scatter(with_other_core([after(p, grad_attn) for p in out_parts]))
        block_out = (resid_mid + mixture).astype(BF16)
        grad_attended = mm_cols(grad_attn, out_here).astype(BF16)
        down_sums = [summed(down_parts[0], grad_moe_in), summed(down_parts[1], grad_attn)]
        up_parts = [over_x(up_first)]
        grad_query, grad_key, grad_value = [], [], []
        for m in range(micro_count):
            query_here, key_here, value_here = [], [], []
            for h in range(heads_here):
                at = micro_rows(m), head_cols(h)
                prob = probs[m, h]
                value_here.append(mm_rows(prob.astype(BF16), grad_attended[at]).astype(BF16))
                grad_pa = mm_cols(grad_attended[at], value[at])
                delta = jnp.sum(prob * grad_pa, axis=-1, keepdims=True)
                grad_scores = (prob * (grad_pa - delta)).astype(BF16)
                query_here.append(mm(grad_scores, key[at]) * score_scale)
                key_here.append(mm_rows(grad_scores, query[at]) * score_scale)
            grad_query.append(jnp.concatenate(query_here, axis=1))
            grad_key.append(jnp.concatenate(key_here, axis=1))
            grad_value.append(jnp.concatenate(value_here, axis=1))
        grad_query = rope_back(jnp.concatenate(grad_query, axis=0))
        grad_key = rope_back(jnp.concatenate(grad_key, axis=0))
        grad_value = jnp.concatenate(grad_value, axis=0)
        inner_query, inner_key = grad_query * gain_query, grad_key * gain_key
        query_gain_grad = jnp.sum(grad_query * query_raw * query_scale, axis=0)
        key_gain_grad = jnp.sum(grad_key * key_raw * key_scale, axis=0)
        means = jnp.stack(
            [jnp.sum(inner_query * query_raw, axis=1), jnp.sum(inner_key * key_raw, axis=1)]
        )
        means = sum_ep(means, y_count, micro_count) / width
        query_back = (
            query_scale * inner_query - query_raw * (query_scale**3 * means[0][:, None])
        ).astype(BF16)
        key_back = (
            key_scale * inner_key - key_raw * (key_scale**3 * means[1][:, None])
        ).astype(BF16)
        raw_grad = jnp.concatenate([query_back, key_back, grad_value], axis=1)
        d_down = both_cores(down_sums, 0)
        normed_part = mm_cols(after(raw_grad, d_down), qkv)
        attn_gain_grad = jnp.sum(normed_part * rows * row_scale, axis=0)
        grad_normed = scatter(normed_part.astype(BF16))
        in_scale = norm_scale(own)
        inner = grad_normed * gain_attn
        d_tokens = (
            grad_mid
            + in_scale * inner
            - own * (in_scale**3 * jnp.mean(own * inner, axis=-1, keepdims=True))
        )

        qkv_grad = mm_rows(normed, raw_grad)
        qkv_kept = keep_core(qkv_grad.reshape(grp_size, -1, 3 * local_width), x_count)
        up_parts.append(over_x(up_second, qkv_kept))
        qkv_grad = keep_x(qkv_kept, x_count)
        gate_sums = [summed(gate_parts[0], raw_grad), summed(gate_parts[1], grad_normed)]
        d_gate = both_cores(gate_sums, 1)
        qkv_grad = after(qkv_grad, d_gate, block_out)
        up_sums = [summed(up_parts[0], grad_normed), summed(up_parts[1], d_gate)]
        d_up = both_cores(up_sums, 1)
        qkv_grad = qkv_grad.astype(BF16).reshape(group_size, weight_rows, 3 * local_width)
        qkv_grad = lax.all_to_all(
            qkv_grad, ("z", "y"), split_axis=0, concat_axis=0, tiled=True
        ).astype(F32)

        def by_row(grads):
            shaped = grads.reshape(head_sets, pieces, weight_rows, heads_here, head_dim)
            return shaped.transpose(2, 1, 3, 0, 4).reshape(weight_rows, width)

        d_query = by_row(qkv_grad[:, :, :local_width])
        d_key = by_row(qkv_grad[:, :, local_width : 2 * local_width])
        d_value = by_row(qkv_grad[:, :, 2 * local_width :])
        out_grad = mm_rows(attended, grad_attn)
        out_grad = keep_x(keep_core(out_grad.reshape(grp_size, weight_rows, width), x_count), x_count)
        d_out = lax.ppermute(
            out_grad.astype(BF16), ALL, [(user, home) for home, user in out_pairs]
        ).astype(F32)

        vectors = jnp.stack(
            [
                attn_gain_grad,
                head_part_back(query_gain_grad),
                head_part_back(key_gain_grad),
                moe_gain_grad,
            ]
        )
        vectors = vectors.reshape(4, device_count, weight_rows).transpose(1, 0, 2)
        small_grads = jnp.concatenate(
            [
                vectors.reshape(device_count, 4 * weight_rows),
                router_grad.reshape(device_count, weight_rows * expert_count),
            ],
            axis=1,
        )
        small_grads = lax.all_to_all(
            after(small_grads, grad_normed, gate_sums), ALL, split_axis=0, concat_axis=0, tiled=True
        )
        small_grads = jnp.sum(small_grads, axis=0)
        gain_grads = small_grads[: 4 * weight_rows].reshape(4, weight_rows)
        d_router = small_grads[4 * weight_rows :].reshape(weight_rows, expert_count)

        shape = (micro_count, seq_parts, row_count, width)
        return (
            block_out.reshape(shape),
            d_tokens.reshape(shape),
            gain_grads[0],
            d_query,
            d_key,
            d_value,
            gain_grads[1],
            gain_grads[2],
            d_out,
            gain_grads[3],
            d_router,
            d_gate,
            d_up,
            d_down,
        )

    return per_device


def solution(mesh):
    devices = mesh.devices
    x_count, y_count, z_count = (
        len({device.coords[axis] for device in devices.flat}) for axis in range(3)
    )
    fine = Mesh(devices.reshape(x_count, 2, z_count, y_count), ALL)
    grp, ep = ("x", "core"), ("z", "y")
    by_token = P(None, grp, ep, None)
    vector, matrix, expert = P(ALL), P(ALL, None), P(ep, None, None)
    return jax.shard_map(
        make_per_device(x_count, z_count, y_count),
        mesh=fine,
        in_specs=(
            by_token,
            by_token,
            vector,
            matrix,
            matrix,
            matrix,
            vector,
            vector,
            matrix,
            vector,
            matrix,
            expert,
            expert,
            expert,
            by_token,
        ),
        out_specs=(
            by_token,
            by_token,
            vector,
            matrix,
            matrix,
            matrix,
            vector,
            vector,
            matrix,
            vector,
            matrix,
            expert,
            expert,
            expert,
        ),
        check_vma=False,
    )
```

```python
import functools
import math

import jax
import jax.numpy as jnp
from jax import lax
from jax.experimental import pallas as pl
from jax.experimental.pallas import tpu as pltpu
from jax.sharding import Mesh, PartitionSpec as P

HEADS = 16
CAP = 36
NORM_EPSILON = 1e-05
ROPE_BASE = 10000.0
ALL = ("x", "core", "z", "y")
SWAP = ((0, 1), (1, 0))
F32 = jnp.float32
BF16 = jnp.bfloat16


def turn(count, step):
    return tuple((i, (i + step) % count) for i in range(count))


def flip(count, bits):
    return tuple((i, i ^ bits) for i in range(count))


def after(values, *others):
    if not others:
        return values
    return lax.optimization_barrier((values,) + others)[0]


def mm(left, right):
    return jnp.dot(left, right, preferred_element_type=F32)


def mm_rows(left, right):
    return lax.dot_general(left, right, (((0,), (0,)), ((), ())), preferred_element_type=F32)


def mm_cols(left, right):
    return lax.dot_general(left, right, (((1,), (1,)), ((), ())), preferred_element_type=F32)


def unturn(items, index):
    count = len(items)
    if count == 1:
        return items
    placed = []
    for place in range(count):
        chosen = items[(0 - place) % count]
        for at in range(1, count):
            chosen = jnp.where(index == at, items[(at - place) % count], chosen)
        placed.append(chosen)
    return placed


def gather_ep(block, y_count, micro_count):
    by_z = {0: block}
    by_z[2] = lax.ppermute(block, "z", flip(4, 2))
    by_z[1] = lax.ppermute(block, "z", flip(4, 1))
    blocks = {}

    def along_y(a):
        blocks[a, 0] = by_z[a]
        for j in range(1, y_count):
            blocks[a, j] = lax.ppermute(by_z[a], "y", flip(y_count, j))

    along_y(0)
    by_z[3] = lax.ppermute(by_z[2], "z", flip(4, 1))
    for a in (1, 2, 3):
        along_y(a)
    rows = block.shape[0] // micro_count
    return jnp.concatenate(
        [
            blocks[a, j][m * rows : (m + 1) * rows]
            for m in range(micro_count)
            for a in range(4)
            for j in range(y_count)
        ],
        axis=0,
    )


def scatter_ep(part, y_count, micro_count):
    rows = part.shape[0] // (4 * y_count * micro_count)

    def piece(a, j):
        starts = [((m * 4 + a) * y_count + j) * rows for m in range(micro_count)]
        return jnp.concatenate([part[at : at + rows] for at in starts], axis=0)

    sums = {}

    def along_y(a):
        total = piece(a, 0).astype(F32)
        for j in range(1, y_count):
            arrived = lax.ppermute(piece(a, j).astype(BF16), "y", flip(y_count, j))
            total = total + arrived.astype(F32)
        sums[a] = total

    along_y(3)
    along_y(2)
    sums[2] = sums[2] + lax.ppermute(sums[3].astype(BF16), "z", flip(4, 1)).astype(F32)
    across = lax.ppermute(sums[2].astype(BF16), "z", flip(4, 2)).astype(F32)
    along_y(1)
    near = lax.ppermute(sums[1].astype(BF16), "z", flip(4, 1)).astype(F32)
    along_y(0)
    return sums[0] + near + across


def sum_ep(values, y_count, micro_count):
    shape = values.shape
    values = values.reshape(shape[0] * micro_count, 4, y_count, -1)

    def moved(source, axis, count, at, bits):
        arrived = lax.ppermute(source, axis, flip(count, bits))
        picked = [lax.index_in_dim(arrived, b ^ bits, at, keepdims=True) for b in range(count)]
        return jnp.concatenate(picked, axis=at)

    along = values
    for j in range(1, y_count):
        along = along + moved(values, "y", y_count, 2, j)
    total = along
    for a in (1, 2, 3):
        total = total + moved(along, "z", 4, 1, a)
    return total.reshape(shape)


def gather_grp(block, x_count):
    x_at, core = lax.axis_index("x"), lax.axis_index("core")
    mine = [block] + [lax.ppermute(block, "x", turn(x_count, i)) for i in range(1, x_count)]
    theirs = [lax.ppermute(item, "core", SWAP) for item in mine]
    mine, theirs = unturn(mine, x_at), unturn(theirs, x_at)
    stacked = []
    for own, other in zip(mine, theirs):
        stacked += [jnp.where(core == 0, own, other), jnp.where(core == 0, other, own)]
    return jnp.stack(stacked)


def keep_core(parts, x_count):
    core = lax.axis_index("core")
    parts = parts.reshape((x_count, 2) + parts.shape[1:])
    away = lax.dynamic_index_in_dim(parts, 1 - core, 1, keepdims=False).astype(BF16)
    kept = lax.dynamic_index_in_dim(parts, core, 1, keepdims=False)
    return kept + lax.ppermute(away, "core", SWAP).astype(F32)


def keep_x(kept, x_count, start=()):
    x_at = lax.axis_index("x")
    total = lax.dynamic_index_in_dim(kept, x_at, 0, keepdims=False)
    for i in range(1, x_count):
        away = lax.dynamic_index_in_dim(kept, (x_at - i) % x_count, 0, keepdims=False)
        arrived = lax.ppermute(away.astype(BF16), "x", turn(x_count, -i))
        total = total + after(arrived, *start).astype(F32)
    return total


def experts_kernel(count, which, hot_ref, router_ref, *refs):
    select, select_t, moe, cot = (refs[i * count : (i + 1) * count] for i in range(4))
    gate_ref, up_ref, down_ref = refs[4 * count : 4 * count + 3]
    rest = refs[4 * count + 3 :]
    grad_out, row_out = rest[:count], rest[count : 2 * count]
    rows_ref, cot_ref, act_ref, dgate_ref, dup_ref, logit_ref = rest[2 * count : 2 * count + 6]
    total_ref, back_ref, prob_ref, weight_ref, share_ref = rest[2 * count + 6 :]
    step = pl.program_id(0)
    slots = select[0].shape[1]

    @pl.when(step == 0)
    def _():
        for i in range(count):
            at = pl.ds(i * slots, slots)
            rows_ref[at, :] = mm(select[i][0], moe[i][...]).astype(BF16)
            cot_ref[at, :] = mm(select[i][0], cot[i][...]).astype(BF16)
        logits = mm(rows_ref[...], router_ref[...])
        lane = lax.broadcasted_iota(jnp.int32, logits.shape, 1)
        logits = jnp.where(lane < which, logits, -1e30)
        logits = jnp.exp(logits - jnp.max(logits, axis=1, keepdims=True))
        prob = logits / jnp.sum(logits, axis=1, keepdims=True)
        prob_ref[...] = prob
        weight = jnp.sum(prob * hot_ref[...], axis=1, keepdims=True)
        weight_ref[...] = jnp.broadcast_to(weight, weight_ref.shape)
        share_ref[...] = jnp.zeros_like(share_ref)

    weight = weight_ref[:, :1]
    gate_w, up_w, down_w = gate_ref[0], up_ref[0], down_ref[0]
    gate = mm(rows_ref[...], gate_w)
    up = mm(rows_ref[...], up_w)
    sigmoid = jax.nn.sigmoid(gate)
    silu = gate * sigmoid
    active = silu * up
    act = (weight * active).astype(BF16)
    act_ref[...] = act
    grad = mm_cols(cot_ref[...], down_w)
    share_ref[...] += jnp.broadcast_to(
        jnp.sum(active * grad, axis=1, keepdims=True), share_ref.shape
    )
    grad = weight * grad
    dup = (grad * silu).astype(BF16)
    dgate = (grad * up * (sigmoid + silu * (1.0 - sigmoid))).astype(BF16)
    dup_ref[...] = dup
    dgate_ref[...] = dgate
    weighted = mm(act, down_w)
    back = mm_cols(dgate, gate_w) + mm_cols(dup, up_w)

    @pl.when(step == 0)
    def _():
        total_ref[...] = weighted
        back_ref[...] = back

    @pl.when(step > 0)
    def _():
        total_ref[...] += weighted
        back_ref[...] += back

    @pl.when(step == pl.num_programs(0) - 1)
    def _():
        logit = (share_ref[...] * weight_ref[...] * (hot_ref[...] - prob_ref[...])).astype(BF16)
        logit_ref[...] = logit
        for i in range(count):
            at = pl.ds(i * slots, slots)
            back = (back_ref[at, :] + mm_cols(logit_ref[at, :], router_ref[...])).astype(BF16)
            grad_out[i][...] = mm(select_t[i][0], back).astype(BF16)
            row_out[i][...] = mm(select_t[i][0], total_ref[at, :].astype(BF16)).astype(BF16)


def run_experts(
    sets, at, hot, router, select, select_t, micro, moe, cot, w_gate, w_up, w_down, experts, hidden
):
    count, (slots, seq_len), width = len(sets), select.shape[1:], router.shape[0]
    block = min(hidden, 512)
    steps, rows = hidden // block, count * slots

    def whole(array):
        return pl.BlockSpec(
            array.shape, lambda f, at: (0,) * array.ndim, pipeline_mode=pl.Buffered(1)
        )

    def kept(shape):
        return pl.BlockSpec(shape, lambda f, at: (0, 0), pipeline_mode=pl.Buffered(1))

    wide = pl.BlockSpec((1, width, block), lambda f, at: (at[0], 0, at[1] + f))
    tall = pl.BlockSpec((1, block, width), lambda f, at: (at[0], at[1] + f, 0))
    hidden_rows = pl.BlockSpec((rows, block), lambda f, at: (0, f))
    one_micro = pl.BlockSpec(
        (seq_len, width), lambda f, at: (micro, 0), pipeline_mode=pl.Buffered(1)
    )
    tables = [array for array in (select, select_t) for _ in sets]
    table_specs = [
        pl.BlockSpec(
            (1,) + array.shape[1:],
            functools.partial(lambda one, f, at: (one, 0, 0), one),
            pipeline_mode=pl.Buffered(1),
        )
        for array in (select, select_t)
        for one in sets
    ]
    one_micro = pl.BlockSpec(
        (seq_len, width), lambda f, at: (micro, 0), pipeline_mode=pl.Buffered(1)
    )
    tables = [array for array in (select, select_t) for _ in sets]
    table_specs = [
        pl.BlockSpec(
            (1,) + array.shape[1:],
            functools.partial(lambda one, f, at: (one, 0, 0), one),
            pipeline_mode=pl.Buffered(1),
        )
        for array in (select, select_t)
        for one in sets
    ]
    tokens = jax.ShapeDtypeStruct((seq_len, width), BF16)
    gathered = jax.ShapeDtypeStruct((rows, width), BF16)
    inner = jax.ShapeDtypeStruct((rows, hidden), BF16)
    result = pl.pallas_call(
        lambda at, *refs: experts_kernel(count, experts, *refs),
        grid_spec=pltpu.PrefetchScalarGridSpec(
            num_scalar_prefetch=1,
            grid=(steps,),
            in_specs=[whole(hot), whole(router)]
            + table_specs
            + [one_micro] * (2 * count)
            + [wide, wide, tall],
            out_specs=[kept((seq_len, width))] * (2 * count)
            + [kept((rows, width))] * 2
            + [hidden_rows] * 3
            + [kept((rows, 128))],
            scratch_shapes=[pltpu.VMEM((rows, width), F32)] * 2
            + [pltpu.VMEM((rows, 128), F32)] * 3,
        ),
        out_shape=[tokens] * (2 * count)
        + [gathered] * 2
        + [inner] * 3
        + [jax.ShapeDtypeStruct((rows, 128), BF16)],
        compiler_params=pltpu.CompilerParams(
            dimension_semantics=("arbitrary",), vmem_limit_bytes=62 * 2**20
        ),
        cost_estimate=pl.CostEstimate(
            flops=12 * rows * hidden * width + 8 * rows * seq_len * width,
            bytes_accessed=6 * hidden * width + 16 * seq_len * width + 8 * rows * width,
            transcendentals=rows * hidden,
        ),
        name="experts",
    )(at, hot, router, *tables, *moe, *cot, w_gate, w_up, w_down)
    return result[:count], result[count : 2 * count], result[2 * count :]


def place_kernel(core_ref, own_ref, other_ref, out_ref):
    @pl.when(core_ref[0] == 0)
    def _():
        out_ref[0] = own_ref[...].astype(F32)
        out_ref[1] = other_ref[...].astype(F32)

    @pl.when(core_ref[0] != 0)
    def _():
        out_ref[0] = other_ref[...].astype(F32)
        out_ref[1] = own_ref[...].astype(F32)


def place_experts(core, own, other):
    rows, columns = own.shape
    block = min(rows, 2**18 // columns)
    half = pl.BlockSpec((block, columns), lambda i, core: (i, 0))
    return pl.pallas_call(
        place_kernel,
        grid_spec=pltpu.PrefetchScalarGridSpec(
            num_scalar_prefetch=1,
            grid=(rows // block,),
            in_specs=[half, half],
            out_specs=pl.BlockSpec((2, block, columns), lambda i, core: (0, i, 0)),
        ),
        out_shape=jax.ShapeDtypeStruct((2, rows, columns), F32),
        compiler_params=pltpu.CompilerParams(
            dimension_semantics=("arbitrary",), vmem_limit_bytes=32 * 2**20
        ),
        cost_estimate=pl.CostEstimate(
            flops=0, bytes_accessed=12 * rows * columns, transcendentals=0
        ),
        name="place",
    )(core[None].astype(jnp.int32), own, other)


def norm_scale(values):
    return lax.rsqrt(jnp.mean(values * values, axis=-1, keepdims=True) + NORM_EPSILON)


def make_per_device(x_count, z_count, y_count):
    group_size = z_count * y_count
    grp_size = 2 * x_count

    assert z_count == 4

    def per_device(
        tokens,
        routes,
        attn_gain,
        w_query,
        w_key,
        w_value,
        query_gain,
        key_gain,
        w_out,
        moe_gain,
        w_router,
        w_gate,
        w_up,
        w_down,
        cotangent,
    ):
        micro_count, seq_parts, row_count, width = tokens.shape
        top_count = routes.shape[3]
        tokens = tokens.reshape(micro_count, row_count, width)
        routes = routes.reshape(micro_count, row_count, top_count)
        cotangent = cotangent.reshape(micro_count, row_count, width)
        expert_count = w_router.shape[1]
        seq_len = row_count * group_size
        head_dim = width // HEADS
        half = head_dim // 2
        score_scale = 1.0 / math.sqrt(head_dim)
        weight_rows = w_query.shape[0]
        pieces = head_dim // weight_rows
        heads_here = grp_size // pieces
        head_sets = group_size // pieces
        local_width = heads_here * head_dim
        x_at, core = lax.axis_index("x"), lax.axis_index("core")
        z_at, y_at = lax.axis_index("z"), lax.axis_index("y")
        ep_at = z_at * y_count + y_at
        set_at, piece_at = ep_at // pieces, ep_at % pieces
        slots = CAP * group_size
        local_experts = w_gate.shape[0]
        ff_width = w_gate.shape[2]

        def gather(block):
            return gather_ep(block.reshape(-1, width), y_count, micro_count)

        def scatter(part):
            return scatter_ep(part, y_count, micro_count)

        def by_owner(weight):
            shaped = weight.reshape(weight_rows, pieces, heads_here, head_sets, head_dim)
            return shaped.transpose(3, 1, 0, 2, 4).reshape(group_size, weight_rows, local_width)

        qkv = jnp.concatenate([by_owner(w) for w in (w_query, w_key, w_value)], axis=2)
        qkv = lax.all_to_all(qkv, ("z", "y"), split_axis=0, concat_axis=0, tiled=True)
        small = jnp.concatenate(
            [w_router]
            + [g[:, None] for g in (attn_gain, query_gain, key_gain, moe_gain)],
            axis=1,
        ).reshape(-1)
        naming = jnp.any(
            routes.reshape(1, -1, top_count)
            == jnp.arange(expert_count, dtype=jnp.int32)[:, None, None],
            axis=-1,
        ).astype(BF16)
        if local_experts == 2:
            naming = naming.reshape(group_size, 2, -1).transpose(1, 0, 2)
        else:
            assert local_experts == 1
            naming = jnp.broadcast_to(naming[None], (2,) + naming.shape)
        device_count = grp_size * group_size
        naming = jnp.broadcast_to(naming[None], (x_count,) + naming.shape).reshape(device_count, -1)
        small = jnp.concatenate(
            [jnp.broadcast_to(small[None], (device_count, small.shape[0])), naming], axis=1
        )
        small = lax.all_to_all(after(small, qkv), ALL, split_axis=0, concat_axis=0, tiled=True)
        named = small[:, -micro_count * row_count :]
        small = small[:, : -micro_count * row_count].reshape(width, expert_count + 4)
        full_router = small[:, :expert_count]
        gains = small[:, expert_count:].astype(F32).T
        gain_attn, gain_query, gain_key, gain_moe = gains[0:1], gains[1], gains[2], gains[3:4]

        def head_part(vector):
            shaped = vector.reshape(pieces, heads_here, head_sets, head_dim)
            shaped = lax.dynamic_index_in_dim(shaped, piece_at, 0, keepdims=False)
            return lax.dynamic_index_in_dim(shaped, set_at, 1, keepdims=False).reshape(1, -1)

        def head_part_back(vector):
            piece_hot = jnp.arange(pieces) == piece_at
            set_hot = jnp.arange(head_sets) == set_at
            hot = piece_hot[:, None, None, None] & set_hot[None, None, :, None]
            return jnp.where(hot, vector.reshape(1, heads_here, 1, head_dim), 0.0).reshape(-1)

        gain_query, gain_key = head_part(gain_query), head_part(gain_key)

        sent_qkv = qkv
        qkv = gather_grp(qkv.reshape(group_size * weight_rows, 3 * local_width), x_count)
        qkv = qkv.reshape(width, 3 * local_width)
        out_pairs = []
        for s in range(head_sets):
            for t in range(pieces):
                for h in range(heads_here):
                    for p in range(pieces):
                        home = (t * heads_here + h) * group_size + s * pieces + p
                        user = (h * pieces + p) * group_size + s * pieces + t
                        out_pairs.append((home, user))
        out_here = lax.ppermute(w_out, ALL, out_pairs)
        out_here = gather_grp(out_here, x_count).reshape(local_width, width)

        z_from = z_at ^ jnp.arange(z_count, dtype=jnp.int32)
        y_from = y_at ^ jnp.arange(y_count, dtype=jnp.int32)
        block_from = z_from[:, None] * y_count + y_from[None, :]
        positions = (
            block_from.reshape(-1)[:, None] * row_count
            + jnp.arange(row_count, dtype=jnp.int32)[None, :]
        ).reshape(-1)
        frequency = jnp.exp(
            -math.log(ROPE_BASE) * jnp.arange(half, dtype=F32) * 2.0 / head_dim
        )
        angles = positions.astype(F32)[:, None] * frequency[None, :]
        cosine, sine = jnp.cos(angles), jnp.sin(angles)
        cos_both = jnp.concatenate([cosine, cosine], axis=1)
        sin_both = jnp.concatenate([-sine, sine], axis=1)
        allowed = positions[:, None] >= positions[None, :]

        def halves_swapped(values):
            parts = []
            for h in range(heads_here):
                at = h * head_dim
                parts += [values[:, at + half : at + head_dim], values[:, at : at + half]]
            return jnp.concatenate(parts, axis=1)

        wide_cos = jnp.tile(cos_both, (micro_count, heads_here))
        wide_sin = jnp.tile(sin_both, (micro_count, heads_here))

        def rope(values):
            return values * wide_cos + halves_swapped(values) * wide_sin

        def rope_back(values):
            return values * wide_cos - halves_swapped(values) * wide_sin

        if local_experts == 2:
            expert_at, hidden = ep_at * 2 + core, ff_width
            expert_place = jnp.stack([core, 0 * core]).astype(jnp.int32)
        else:
            expert_at, hidden = ep_at, ff_width // 2
            expert_place = jnp.stack([0 * core, core]).astype(jnp.int32)
        hot = (jnp.arange(128, dtype=jnp.int32) == expert_at).astype(F32)[None]
        padded_router = jnp.pad(full_router, ((0, 0), (0, 128 - expert_count)))

        named = named.reshape((x_count, 2, z_count, y_count, micro_count, row_count))
        named = lax.dynamic_index_in_dim(named, x_at, 0, keepdims=False)
        named = jnp.where(core == 0, named, named[::-1])
        named = jnp.take(jnp.take(named, z_from, axis=1), y_from, axis=2)
        named = named.transpose(3, 0, 1, 2, 4).reshape(2 * micro_count, seq_len) > 0.5
        earlier = jnp.arange(seq_len)[:, None] < jnp.arange(seq_len)[None, :]
        rank = mm(named.astype(BF16), earlier.astype(BF16)).astype(jnp.int32)
        rank = jnp.where(named, rank, -1)
        slot_ids = jnp.arange(slots, dtype=jnp.int32)
        select = (rank[:, None, :] == slot_ids[None, :, None]).astype(BF16)
        select_t = (rank[:, :, None] == slot_ids[None, None, :]).astype(BF16)

        def micro_rows(m):
            return slice(m * seq_len, (m + 1) * seq_len)

        def head_cols(h):
            return slice(h * head_dim, (h + 1) * head_dim)

        own = tokens.reshape(-1, width).astype(F32)
        micros = range(micro_count)
        rows = gather(tokens)
        low_rows = rows
        rows = rows.astype(F32)
        row_scale = norm_scale(rows)
        normed = (rows * row_scale * gain_attn).astype(BF16)
        raw = mm(normed, qkv)
        query_raw, key_raw = raw[:, :local_width], raw[:, local_width : 2 * local_width]
        value = raw[:, 2 * local_width :].astype(BF16)
        squares = jnp.stack(
            [jnp.sum(query_raw * query_raw, axis=1), jnp.sum(key_raw * key_raw, axis=1)]
        )
        squares = sum_ep(squares, y_count, micro_count)
        cot_all = [gather(after(cotangent, sent_qkv))]
        scales = lax.rsqrt(squares / width + NORM_EPSILON)
        query_scale, key_scale = scales[0][:, None], scales[1][:, None]
        query = rope(query_raw * query_scale * gain_query).astype(BF16)
        key = rope(key_raw * key_scale * gain_key).astype(BF16)
        probs, attended = {}, []
        for m in range(micro_count):
            here = []
            for h in range(heads_here):
                at = micro_rows(m), head_cols(h)
                scores = mm_cols(query[at], key[at]) * score_scale
                scores = jnp.where(allowed, scores, -1e30)
                scores = jnp.exp(scores - jnp.max(scores, axis=-1, keepdims=True))
                prob = scores / jnp.sum(scores, axis=-1, keepdims=True)
                probs[m, h] = prob
                here.append(mm(prob.astype(BF16), value[at]).astype(BF16))
            attended.append(jnp.concatenate(here, axis=1))
        attended = jnp.concatenate(attended, axis=0)
        resid_mid = own + scatter(mm(attended, out_here).astype(BF16))

        def with_other_core(parts):
            arrived = [lax.ppermute(p[1], "core", SWAP) for p in parts]
            return jnp.concatenate(
                [
                    (p[0].astype(F32) + other.astype(F32)).astype(BF16)
                    for p, other in zip(parts, arrived)
                ],
                axis=0,
            )

        moe_scale = norm_scale(resid_mid)
        moe_all = [gather((resid_mid * moe_scale * gain_moe).astype(BF16))]
        moe_all.append(lax.ppermute(moe_all[0], "core", SWAP))
        cot_all.append(lax.ppermute(cot_all[0], "core", SWAP))
        saved, out_parts, grad_parts = [], [], []
        for m in micros:
            sets = [slice(0, 2)] if slots <= 288 else [slice(0, 1), slice(1, 2)]
            grads, outs = [], []
            for here in sets:
                grad, out, rest = run_experts(
                    range(2 * m, 2 * m + 2)[here],
                    expert_place,
                    hot,
                    padded_router,
                    select,
                    select_t,
                    m,
                    moe_all[here],
                    cot_all[here],
                    w_gate,
                    w_up,
                    w_down,
                    expert_count,
                    hidden,
                )
                grads, outs = grads + list(grad), outs + list(out)
                saved.append(rest)
            grad_parts.append(grads)
            out_parts.append(outs)
        grad_sum = with_other_core(grad_parts)
        grad_moe_in = scatter(grad_sum)

        def over_pairs(left, right):
            total = None
            for rest in saved:
                term = mm_rows(rest[left], rest[right])
                total = term if total is None else total + term
            return total

        def over_x(low, start=None):
            sent = low if start is None else after(low, start)
            return [low] + [
                lax.ppermute(sent, "x", turn(x_count, i)) for i in range(1, x_count)
            ]

        def summed(parts, start):
            parts = [parts[0]] + [after(p, start) for p in parts[1:]]
            if x_count > 2:
                parts = unturn(parts, x_at)
            total = parts[0].astype(F32)
            for item in parts[1:]:
                total = total + item.astype(F32)
            return total.astype(BF16)

        def both_cores(own_part, axis):
            other = lax.ppermute(own_part, "core", SWAP)
            if local_experts == 2:
                return place_experts(core, own_part, other)
            first = jnp.where(core == 0, own_part, other)
            second = jnp.where(core == 0, other, own_part)
            return jnp.concatenate([first, second], axis=axis)[None].astype(F32)

        down_low = over_pairs(2, 1).astype(BF16)
        saved = [[after(r, grad_sum) for r in rest] for rest in saved]
        gate_low = over_pairs(0, 3).astype(BF16)
        up_low = over_pairs(0, 4).astype(BF16)
        router_grad = over_pairs(0, 5)[:, :expert_count]
        down_parts, gate_parts = over_x(down_low), over_x(gate_low)

        grad_out = cotangent.reshape(-1, width).astype(F32)
        moe_gain_grad = jnp.sum(grad_moe_in * resid_mid * moe_scale, axis=0)
        inner = grad_moe_in * gain_moe
        grad_mid = (
            grad_out
            + moe_scale * inner
            - resid_mid * (moe_scale**3 * jnp.mean(resid_mid * inner, axis=-1, keepdims=True))
        )
        grad_attn = gather(grad_mid.astype(BF16))
        mixture = scatter(after(with_other_core(out_parts), grad_attn))
        block_out = (resid_mid + mixture).astype(BF16)
        grad_attended = mm_cols(grad_attn, out_here).astype(BF16)
        down_sum = summed(down_parts, grad_attn)
        up_parts = over_x(up_low, grad_attn)
        grad_query, grad_key, grad_value = [], [], []
        for m in range(micro_count):
            query_here, key_here, value_here = [], [], []
            for h in range(heads_here):
                at = micro_rows(m), head_cols(h)
                prob = probs[m, h]
                value_here.append(mm_rows(prob.astype(BF16), grad_attended[at]).astype(BF16))
                grad_pa = mm_cols(grad_attended[at], value[at])
                delta = jnp.sum(prob * grad_pa, axis=-1, keepdims=True)
                grad_scores = (prob * (grad_pa - delta)).astype(BF16)
                query_here.append(mm(grad_scores, key[at]) * score_scale)
                key_here.append(mm_rows(grad_scores, query[at]) * score_scale)
            grad_query.append(jnp.concatenate(query_here, axis=1))
            grad_key.append(jnp.concatenate(key_here, axis=1))
            grad_value.append(jnp.concatenate(value_here, axis=1))
        grad_query = rope_back(jnp.concatenate(grad_query, axis=0))
        grad_key = rope_back(jnp.concatenate(grad_key, axis=0))
        grad_value = jnp.concatenate(grad_value, axis=0)
        inner_query, inner_key = grad_query * gain_query, grad_key * gain_key
        query_gain_grad = jnp.sum(grad_query * query_raw * query_scale, axis=0)
        key_gain_grad = jnp.sum(grad_key * key_raw * key_scale, axis=0)
        means = jnp.stack(
            [jnp.sum(inner_query * query_raw, axis=1), jnp.sum(inner_key * key_raw, axis=1)]
        )
        means = sum_ep(means, y_count, micro_count) / width
        query_back = (
            query_scale * inner_query - query_raw * (query_scale**3 * means[0][:, None])
        ).astype(BF16)
        key_back = (
            key_scale * inner_key - key_raw * (key_scale**3 * means[1][:, None])
        ).astype(BF16)
        raw_grad = jnp.concatenate([after(query_back, block_out), key_back, grad_value], axis=1)
        d_down = both_cores(down_sum, 0)
        gate_sum = summed(gate_parts, raw_grad)
        normed_part = mm_cols(after(raw_grad, d_down), qkv)
        attn_gain_grad = jnp.sum(normed_part * rows * row_scale, axis=0)
        grad_normed = scatter(normed_part.astype(BF16))
        in_scale = norm_scale(own)
        inner = grad_normed * gain_attn
        d_tokens = (
            grad_mid
            + in_scale * inner
            - own * (in_scale**3 * jnp.mean(own * inner, axis=-1, keepdims=True))
        )

        qkv_grad = mm_rows(normed, raw_grad)
        qkv_kept = keep_core(qkv_grad.reshape(grp_size, -1, 3 * local_width), x_count)
        qkv_grad = keep_x(qkv_kept, x_count, (grad_normed,))
        d_gate = both_cores(gate_sum, 1)
        qkv_grad = after(qkv_grad, d_gate, block_out)
        up_sum = summed(up_parts, grad_normed)
        d_up = both_cores(up_sum, 1)
        qkv_grad = qkv_grad.astype(BF16).reshape(group_size, weight_rows, 3 * local_width)
        qkv_grad = lax.all_to_all(
            qkv_grad, ("z", "y"), split_axis=0, concat_axis=0, tiled=True
        ).astype(F32)

        def by_row(grads):
            shaped = grads.reshape(head_sets, pieces, weight_rows, heads_here, head_dim)
            return shaped.transpose(2, 1, 3, 0, 4).reshape(weight_rows, width)

        d_query = by_row(qkv_grad[:, :, :local_width])
        d_key = by_row(qkv_grad[:, :, local_width : 2 * local_width])
        d_value = by_row(qkv_grad[:, :, 2 * local_width :])
        out_grad = mm_rows(attended, grad_attn)
        out_grad = keep_x(keep_core(out_grad.reshape(grp_size, weight_rows, width), x_count), x_count)
        d_out = lax.ppermute(
            out_grad.astype(BF16), ALL, [(user, home) for home, user in out_pairs]
        ).astype(F32)

        vectors = jnp.stack(
            [
                attn_gain_grad,
                head_part_back(query_gain_grad),
                head_part_back(key_gain_grad),
                moe_gain_grad,
            ]
        )
        vectors = vectors.reshape(4, device_count, weight_rows).transpose(1, 0, 2)
        small_grads = jnp.concatenate(
            [
                vectors.reshape(device_count, 4 * weight_rows),
                router_grad.reshape(device_count, weight_rows * expert_count),
            ],
            axis=1,
        )
        small_grads = lax.all_to_all(
            after(small_grads, grad_normed, gate_sum), ALL, split_axis=0, concat_axis=0, tiled=True
        )
        small_grads = jnp.sum(small_grads, axis=0)
        gain_grads = small_grads[: 4 * weight_rows].reshape(4, weight_rows)
        d_router = small_grads[4 * weight_rows :].reshape(weight_rows, expert_count)

        shape = (micro_count, seq_parts, row_count, width)
        return (
            block_out.reshape(shape),
            d_tokens.reshape(shape),
            gain_grads[0],
            d_query,
            d_key,
            d_value,
            gain_grads[1],
            gain_grads[2],
            d_out,
            gain_grads[3],
            d_router,
            d_gate,
            d_up,
            d_down,
        )

    return per_device


def solution(mesh):
    devices = mesh.devices
    x_count, y_count, z_count = (
        len({device.coords[axis] for device in devices.flat}) for axis in range(3)
    )
    fine = Mesh(devices.reshape(x_count, 2, z_count, y_count), ALL)
    grp, ep = ("x", "core"), ("z", "y")
    by_token = P(None, grp, ep, None)
    vector, matrix, expert = P(ALL), P(ALL, None), P(ep, None, None)
    return jax.shard_map(
        make_per_device(x_count, z_count, y_count),
        mesh=fine,
        in_specs=(
            by_token,
            by_token,
            vector,
            matrix,
            matrix,
            matrix,
            vector,
            vector,
            matrix,
            vector,
            matrix,
            expert,
            expert,
            expert,
            by_token,
        ),
        out_specs=(
            by_token,
            by_token,
            vector,
            matrix,
            matrix,
            matrix,
            vector,
            vector,
            matrix,
            vector,
            matrix,
            expert,
            expert,
            expert,
        ),
        check_vma=False,
    )
```

```python
import functools
import math

import jax
import jax.numpy as jnp
from jax import lax
from jax.experimental import pallas as pl
from jax.experimental.pallas import tpu as pltpu
from jax.sharding import Mesh, PartitionSpec as P

HEADS = 16
CAP = 36
NORM_EPSILON = 1e-05
ROPE_BASE = 10000.0
ALL = ("x", "core", "z", "y")
SWAP = ((0, 1), (1, 0))
F32 = jnp.float32
BF16 = jnp.bfloat16


def turn(count, step):
    return tuple((i, (i + step) % count) for i in range(count))


def flip(count, bits):
    return tuple((i, i ^ bits) for i in range(count))


def after(values, *others):
    if not others:
        return values
    return lax.optimization_barrier((values,) + others)[0]


def mm(left, right):
    return jnp.dot(left, right, preferred_element_type=F32)


def mm_rows(left, right):
    return lax.dot_general(left, right, (((0,), (0,)), ((), ())), preferred_element_type=F32)


def mm_cols(left, right):
    return lax.dot_general(left, right, (((1,), (1,)), ((), ())), preferred_element_type=F32)


def unturn(items, index):
    count = len(items)
    if count == 1:
        return items
    placed = []
    for place in range(count):
        chosen = items[(0 - place) % count]
        for at in range(1, count):
            chosen = jnp.where(index == at, items[(at - place) % count], chosen)
        placed.append(chosen)
    return placed


def gather_ep(block, y_count, micro_count):
    by_z = {0: block}
    by_z[2] = lax.ppermute(block, "z", flip(4, 2))
    by_z[1] = lax.ppermute(block, "z", flip(4, 1))
    blocks = {}

    def along_y(a):
        blocks[a, 0] = by_z[a]
        for j in range(1, y_count):
            blocks[a, j] = lax.ppermute(by_z[a], "y", flip(y_count, j))

    along_y(0)
    by_z[3] = lax.ppermute(by_z[2], "z", flip(4, 1))
    for a in (1, 2, 3):
        along_y(a)
    rows = block.shape[0] // micro_count
    return [
        jnp.concatenate(
            [
                blocks[a, j][m * rows : (m + 1) * rows]
                for a in range(4)
                for j in range(y_count)
            ],
            axis=0,
        )
        for m in range(micro_count)
    ]


def scatter_ep(part, y_count, micro_count):
    rows = part.shape[0] // (4 * y_count * micro_count)

    def piece(a, j):
        starts = [((m * 4 + a) * y_count + j) * rows for m in range(micro_count)]
        return jnp.concatenate([part[at : at + rows] for at in starts], axis=0)

    sums = {}

    def along_y(a):
        total = piece(a, 0).astype(F32)
        for j in range(1, y_count):
            arrived = lax.ppermute(piece(a, j).astype(BF16), "y", flip(y_count, j))
            total = total + arrived.astype(F32)
        sums[a] = total

    along_y(3)
    along_y(2)
    sums[2] = sums[2] + lax.ppermute(sums[3].astype(BF16), "z", flip(4, 1)).astype(F32)
    across = lax.ppermute(sums[2].astype(BF16), "z", flip(4, 2)).astype(F32)
    along_y(1)
    near = lax.ppermute(sums[1].astype(BF16), "z", flip(4, 1)).astype(F32)
    along_y(0)
    return sums[0] + near + across


def sum_ep(values, y_count, micro_count):
    shape = values.shape
    values = values.reshape(shape[0] * micro_count, 4, y_count, -1)

    def moved(source, axis, count, at, bits):
        arrived = lax.ppermute(source, axis, flip(count, bits))
        picked = [lax.index_in_dim(arrived, b ^ bits, at, keepdims=True) for b in range(count)]
        return jnp.concatenate(picked, axis=at)

    along = values
    for j in range(1, y_count):
        along = along + moved(values, "y", y_count, 2, j)
    total = along
    for a in (1, 2, 3):
        total = total + moved(along, "z", 4, 1, a)
    return total.reshape(shape)


def gather_grp(block, x_count):
    x_at, core = lax.axis_index("x"), lax.axis_index("core")
    mine = [block] + [lax.ppermute(block, "x", turn(x_count, i)) for i in range(1, x_count)]
    theirs = [lax.ppermute(item, "core", SWAP) for item in mine]
    mine, theirs = unturn(mine, x_at), unturn(theirs, x_at)
    stacked = []
    for own, other in zip(mine, theirs):
        stacked += [jnp.where(core == 0, own, other), jnp.where(core == 0, other, own)]
    return jnp.stack(stacked)


def keep_core(parts, x_count):
    core = lax.axis_index("core")
    parts = parts.reshape((x_count, 2) + parts.shape[1:])
    away = lax.dynamic_index_in_dim(parts, 1 - core, 1, keepdims=False).astype(BF16)
    kept = lax.dynamic_index_in_dim(parts, core, 1, keepdims=False)
    return kept + lax.ppermute(away, "core", SWAP).astype(F32)


def keep_x(kept, x_count, start=()):
    x_at = lax.axis_index("x")
    total = lax.dynamic_index_in_dim(kept, x_at, 0, keepdims=False)
    for i in range(1, x_count):
        away = lax.dynamic_index_in_dim(kept, (x_at - i) % x_count, 0, keepdims=False)
        arrived = lax.ppermute(away.astype(BF16), "x", turn(x_count, -i))
        total = total + after(arrived, *start).astype(F32)
    return total


def experts_kernel(count, which, hot_ref, router_ref, *refs):
    select, select_t, moe, cot = (refs[i * count : (i + 1) * count] for i in range(4))
    gate_ref, up_ref, down_ref = refs[4 * count : 4 * count + 3]
    rest = refs[4 * count + 3 :]
    grad_out, row_out = rest[:count], rest[count : 2 * count]
    rows_ref, cot_ref, act_ref, dgate_ref, dup_ref, logit_ref = rest[2 * count : 2 * count + 6]
    total_ref, back_ref, prob_ref, weight_ref, share_ref = rest[2 * count + 6 :]
    step = pl.program_id(0)
    slots = select[0].shape[1]

    @pl.when(step == 0)
    def _():
        for i in range(count):
            at = pl.ds(i * slots, slots)
            rows_ref[at, :] = mm(select[i][0], moe[i][...]).astype(BF16)
            cot_ref[at, :] = mm(select[i][0], cot[i][...]).astype(BF16)
        logits = mm(rows_ref[...], router_ref[...])
        lane = lax.broadcasted_iota(jnp.int32, logits.shape, 1)
        logits = jnp.where(lane < which, logits, -1e30)
        logits = jnp.exp(logits - jnp.max(logits, axis=1, keepdims=True))
        prob = logits / jnp.sum(logits, axis=1, keepdims=True)
        prob_ref[...] = prob
        weight = jnp.sum(prob * hot_ref[...], axis=1, keepdims=True)
        weight_ref[...] = jnp.broadcast_to(weight, weight_ref.shape)
        share_ref[...] = jnp.zeros_like(share_ref)

    weight = weight_ref[:, :1]
    gate_w, up_w, down_w = gate_ref[0], up_ref[0], down_ref[0]
    gate = mm(rows_ref[...], gate_w)
    up = mm(rows_ref[...], up_w)
    sigmoid = jax.nn.sigmoid(gate)
    silu = gate * sigmoid
    active = silu * up
    act = (weight * active).astype(BF16)
    act_ref[...] = act
    grad = mm_cols(cot_ref[...], down_w)
    share_ref[...] += jnp.broadcast_to(
        jnp.sum(active * grad, axis=1, keepdims=True), share_ref.shape
    )
    grad = weight * grad
    dup = (grad * silu).astype(BF16)
    dgate = (grad * up * (sigmoid + silu * (1.0 - sigmoid))).astype(BF16)
    dup_ref[...] = dup
    dgate_ref[...] = dgate
    weighted = mm(act, down_w)
    back = mm_cols(dgate, gate_w) + mm_cols(dup, up_w)

    @pl.when(step == 0)
    def _():
        total_ref[...] = weighted
        back_ref[...] = back

    @pl.when(step > 0)
    def _():
        total_ref[...] += weighted
        back_ref[...] += back

    @pl.when(step == pl.num_programs(0) - 1)
    def _():
        logit = (share_ref[...] * weight_ref[...] * (hot_ref[...] - prob_ref[...])).astype(BF16)
        logit_ref[...] = logit
        for i in range(count):
            at = pl.ds(i * slots, slots)
            back = (back_ref[at, :] + mm_cols(logit_ref[at, :], router_ref[...])).astype(BF16)
            grad_out[i][...] = mm(select_t[i][0], back).astype(BF16)
            row_out[i][...] = mm(select_t[i][0], total_ref[at, :].astype(BF16)).astype(BF16)


def run_experts(
    sets, at, hot, router, select, select_t, moe, cot, w_gate, w_up, w_down, experts, hidden
):
    count, (slots, seq_len), width = len(sets), select.shape[1:], router.shape[0]
    block = min(hidden, 512)
    steps, rows = hidden // block, count * slots

    def whole(array):
        return pl.BlockSpec(
            array.shape, lambda f, at: (0,) * array.ndim, pipeline_mode=pl.Buffered(1)
        )

    def kept(shape):
        return pl.BlockSpec(shape, lambda f, at: (0, 0), pipeline_mode=pl.Buffered(1))

    wide = pl.BlockSpec((1, width, block), lambda f, at: (at[0], 0, at[1] + f))
    tall = pl.BlockSpec((1, block, width), lambda f, at: (at[0], at[1] + f, 0))
    hidden_rows = pl.BlockSpec((rows, block), lambda f, at: (0, f))
    tables = [array for array in (select, select_t) for _ in sets]
    table_specs = [
        pl.BlockSpec(
            (1,) + array.shape[1:],
            functools.partial(lambda one, f, at: (one, 0, 0), one),
            pipeline_mode=pl.Buffered(1),
        )
        for array in (select, select_t)
        for one in sets
    ]
    one_micro = pl.BlockSpec(
        (seq_len, width), lambda f, at: (micro, 0), pipeline_mode=pl.Buffered(1)
    )
    tables = [array for array in (select, select_t) for _ in sets]
    table_specs = [
        pl.BlockSpec(
            (1,) + array.shape[1:],
            functools.partial(lambda one, f, at: (one, 0, 0), one),
            pipeline_mode=pl.Buffered(1),
        )
        for array in (select, select_t)
        for one in sets
    ]
    tokens = jax.ShapeDtypeStruct((seq_len, width), BF16)
    gathered = jax.ShapeDtypeStruct((rows, width), BF16)
    inner = jax.ShapeDtypeStruct((rows, hidden), BF16)
    result = pl.pallas_call(
        lambda at, *refs: experts_kernel(count, experts, *refs),
        grid_spec=pltpu.PrefetchScalarGridSpec(
            num_scalar_prefetch=1,
            grid=(steps,),
            in_specs=[whole(hot), whole(router)]
            + table_specs
            + [whole(a) for a in (*moe, *cot)]
            + [wide, wide, tall],
            out_specs=[kept((seq_len, width))] * (2 * count)
            + [kept((rows, width))] * 2
            + [hidden_rows] * 3
            + [kept((rows, 128))],
            scratch_shapes=[pltpu.VMEM((rows, width), F32)] * 2
            + [pltpu.VMEM((rows, 128), F32)] * 3,
        ),
        out_shape=[tokens] * (2 * count)
        + [gathered] * 2
        + [inner] * 3
        + [jax.ShapeDtypeStruct((rows, 128), BF16)],
        compiler_params=pltpu.CompilerParams(
            dimension_semantics=("arbitrary",), vmem_limit_bytes=62 * 2**20
        ),
        cost_estimate=pl.CostEstimate(
            flops=12 * rows * hidden * width + 8 * rows * seq_len * width,
            bytes_accessed=6 * hidden * width + 16 * seq_len * width + 8 * rows * width,
            transcendentals=rows * hidden,
        ),
        name="experts",
    )(at, hot, router, *tables, *moe, *cot, w_gate, w_up, w_down)
    return result[:count], result[count : 2 * count], result[2 * count :]


def place_kernel(core_ref, own_ref, other_ref, out_ref):
    @pl.when(core_ref[0] == 0)
    def _():
        out_ref[0] = own_ref[...].astype(F32)
        out_ref[1] = other_ref[...].astype(F32)

    @pl.when(core_ref[0] != 0)
    def _():
        out_ref[0] = other_ref[...].astype(F32)
        out_ref[1] = own_ref[...].astype(F32)


def place_experts(core, own, other):
    rows, columns = own.shape
    block = min(rows, 2**18 // columns)
    half = pl.BlockSpec((block, columns), lambda i, core: (i, 0))
    return pl.pallas_call(
        place_kernel,
        grid_spec=pltpu.PrefetchScalarGridSpec(
            num_scalar_prefetch=1,
            grid=(rows // block,),
            in_specs=[half, half],
            out_specs=pl.BlockSpec((2, block, columns), lambda i, core: (0, i, 0)),
        ),
        out_shape=jax.ShapeDtypeStruct((2, rows, columns), F32),
        compiler_params=pltpu.CompilerParams(
            dimension_semantics=("arbitrary",), vmem_limit_bytes=32 * 2**20
        ),
        cost_estimate=pl.CostEstimate(
            flops=0, bytes_accessed=12 * rows * columns, transcendentals=0
        ),
        name="place",
    )(core[None].astype(jnp.int32), own, other)


def norm_scale(values):
    return lax.rsqrt(jnp.mean(values * values, axis=-1, keepdims=True) + NORM_EPSILON)


def make_per_device(x_count, z_count, y_count):
    group_size = z_count * y_count
    grp_size = 2 * x_count

    assert z_count == 4

    def per_device(
        tokens,
        routes,
        attn_gain,
        w_query,
        w_key,
        w_value,
        query_gain,
        key_gain,
        w_out,
        moe_gain,
        w_router,
        w_gate,
        w_up,
        w_down,
        cotangent,
    ):
        micro_count, seq_parts, row_count, width = tokens.shape
        top_count = routes.shape[3]
        tokens = tokens.reshape(micro_count, row_count, width)
        routes = routes.reshape(micro_count, row_count, top_count)
        cotangent = cotangent.reshape(micro_count, row_count, width)
        expert_count = w_router.shape[1]
        seq_len = row_count * group_size
        head_dim = width // HEADS
        half = head_dim // 2
        score_scale = 1.0 / math.sqrt(head_dim)
        weight_rows = w_query.shape[0]
        pieces = head_dim // weight_rows
        heads_here = grp_size // pieces
        head_sets = group_size // pieces
        local_width = heads_here * head_dim
        x_at, core = lax.axis_index("x"), lax.axis_index("core")
        z_at, y_at = lax.axis_index("z"), lax.axis_index("y")
        ep_at = z_at * y_count + y_at
        set_at, piece_at = ep_at // pieces, ep_at % pieces
        slots = CAP * group_size
        local_experts = w_gate.shape[0]
        ff_width = w_gate.shape[2]

        def gather_micros(block):
            return gather_ep(block.reshape(-1, width), y_count, micro_count)

        def gather(block):
            return jnp.concatenate(gather_micros(block), axis=0)

        def scatter(part):
            return scatter_ep(part, y_count, micro_count)

        def by_owner(weight):
            shaped = weight.reshape(weight_rows, pieces, heads_here, head_sets, head_dim)
            return shaped.transpose(3, 1, 0, 2, 4).reshape(group_size, weight_rows, local_width)

        qkv = jnp.concatenate([by_owner(w) for w in (w_query, w_key, w_value)], axis=2)
        qkv = lax.all_to_all(qkv, ("z", "y"), split_axis=0, concat_axis=0, tiled=True)
        small = jnp.concatenate(
            [w_router]
            + [g[:, None] for g in (attn_gain, query_gain, key_gain, moe_gain)],
            axis=1,
        ).reshape(-1)
        naming = jnp.any(
            routes.reshape(1, -1, top_count)
            == jnp.arange(expert_count, dtype=jnp.int32)[:, None, None],
            axis=-1,
        ).astype(BF16)
        if local_experts == 2:
            naming = naming.reshape(group_size, 2, -1).transpose(1, 0, 2)
        else:
            assert local_experts == 1
            naming = jnp.broadcast_to(naming[None], (2,) + naming.shape)
        device_count = grp_size * group_size
        naming = jnp.broadcast_to(naming[None], (x_count,) + naming.shape).reshape(device_count, -1)
        small = jnp.concatenate(
            [jnp.broadcast_to(small[None], (device_count, small.shape[0])), naming], axis=1
        )
        small = lax.all_to_all(after(small, qkv), ALL, split_axis=0, concat_axis=0, tiled=True)
        named = small[:, -micro_count * row_count :]
        small = small[:, : -micro_count * row_count].reshape(width, expert_count + 4)
        full_router = small[:, :expert_count]
        gains = small[:, expert_count:].astype(F32).T
        gain_attn, gain_query, gain_key, gain_moe = gains[0:1], gains[1], gains[2], gains[3:4]

        def head_part(vector):
            shaped = vector.reshape(pieces, heads_here, head_sets, head_dim)
            shaped = lax.dynamic_index_in_dim(shaped, piece_at, 0, keepdims=False)
            return lax.dynamic_index_in_dim(shaped, set_at, 1, keepdims=False).reshape(1, -1)

        def head_part_back(vector):
            piece_hot = jnp.arange(pieces) == piece_at
            set_hot = jnp.arange(head_sets) == set_at
            hot = piece_hot[:, None, None, None] & set_hot[None, None, :, None]
            return jnp.where(hot, vector.reshape(1, heads_here, 1, head_dim), 0.0).reshape(-1)

        gain_query, gain_key = head_part(gain_query), head_part(gain_key)

        sent_qkv = qkv
        qkv = gather_grp(qkv.reshape(group_size * weight_rows, 3 * local_width), x_count)
        qkv = qkv.reshape(width, 3 * local_width)
        out_pairs = []
        for s in range(head_sets):
            for t in range(pieces):
                for h in range(heads_here):
                    for p in range(pieces):
                        home = (t * heads_here + h) * group_size + s * pieces + p
                        user = (h * pieces + p) * group_size + s * pieces + t
                        out_pairs.append((home, user))
        out_here = lax.ppermute(w_out, ALL, out_pairs)
        out_here = gather_grp(out_here, x_count).reshape(local_width, width)

        z_from = z_at ^ jnp.arange(z_count, dtype=jnp.int32)
        y_from = y_at ^ jnp.arange(y_count, dtype=jnp.int32)
        block_from = z_from[:, None] * y_count + y_from[None, :]
        positions = (
            block_from.reshape(-1)[:, None] * row_count
            + jnp.arange(row_count, dtype=jnp.int32)[None, :]
        ).reshape(-1)
        frequency = jnp.exp(
            -math.log(ROPE_BASE) * jnp.arange(half, dtype=F32) * 2.0 / head_dim
        )
        angles = positions.astype(F32)[:, None] * frequency[None, :]
        cosine, sine = jnp.cos(angles), jnp.sin(angles)
        cos_both = jnp.concatenate([cosine, cosine], axis=1)
        sin_both = jnp.concatenate([-sine, sine], axis=1)
        allowed = positions[:, None] >= positions[None, :]

        def halves_swapped(values):
            parts = []
            for h in range(heads_here):
                at = h * head_dim
                parts += [values[:, at + half : at + head_dim], values[:, at : at + half]]
            return jnp.concatenate(parts, axis=1)

        wide_cos = jnp.tile(cos_both, (micro_count, heads_here))
        wide_sin = jnp.tile(sin_both, (micro_count, heads_here))

        def rope(values):
            return values * wide_cos + halves_swapped(values) * wide_sin

        def rope_back(values):
            return values * wide_cos - halves_swapped(values) * wide_sin

        if local_experts == 2:
            expert_at, hidden = ep_at * 2 + core, ff_width
            expert_place = jnp.stack([core, 0 * core]).astype(jnp.int32)
        else:
            expert_at, hidden = ep_at, ff_width // 2
            expert_place = jnp.stack([0 * core, core]).astype(jnp.int32)
        hot = (jnp.arange(128, dtype=jnp.int32) == expert_at).astype(F32)[None]
        padded_router = jnp.pad(full_router, ((0, 0), (0, 128 - expert_count)))

        named = named.reshape((x_count, 2, z_count, y_count, micro_count, row_count))
        named = lax.dynamic_index_in_dim(named, x_at, 0, keepdims=False)
        named = jnp.where(core == 0, named, named[::-1])
        named = jnp.take(jnp.take(named, z_from, axis=1), y_from, axis=2)
        named = named.transpose(3, 0, 1, 2, 4).reshape(2 * micro_count, seq_len) > 0.5
        earlier = jnp.arange(seq_len)[:, None] < jnp.arange(seq_len)[None, :]
        rank = mm(named.astype(BF16), earlier.astype(BF16)).astype(jnp.int32)
        rank = jnp.where(named, rank, -1)
        slot_ids = jnp.arange(slots, dtype=jnp.int32)
        select = (rank[:, None, :] == slot_ids[None, :, None]).astype(BF16)
        select_t = (rank[:, :, None] == slot_ids[None, None, :]).astype(BF16)

        def micro_rows(m):
            return slice(m * seq_len, (m + 1) * seq_len)

        def head_cols(h):
            return slice(h * head_dim, (h + 1) * head_dim)

        own = tokens.reshape(-1, width).astype(F32)
        micros = range(micro_count)
        rows = gather(tokens)
        low_rows = rows
        rows = rows.astype(F32)
        row_scale = norm_scale(rows)
        normed = (rows * row_scale * gain_attn).astype(BF16)
        raw = mm(normed, qkv)
        query_raw, key_raw = raw[:, :local_width], raw[:, local_width : 2 * local_width]
        value = raw[:, 2 * local_width :].astype(BF16)
        squares = jnp.stack(
            [jnp.sum(query_raw * query_raw, axis=1), jnp.sum(key_raw * key_raw, axis=1)]
        )
        squares = sum_ep(squares, y_count, micro_count)
        cot_own = gather_micros(after(cotangent, sent_qkv))
        scales = lax.rsqrt(squares / width + NORM_EPSILON)
        query_scale, key_scale = scales[0][:, None], scales[1][:, None]
        query = rope(query_raw * query_scale * gain_query).astype(BF16)
        key = rope(key_raw * key_scale * gain_key).astype(BF16)
        probs, attended = {}, []
        for m in range(micro_count):
            here = []
            for h in range(heads_here):
                at = micro_rows(m), head_cols(h)
                scores = mm_cols(query[at], key[at]) * score_scale
                scores = jnp.where(allowed, scores, -1e30)
                scores = jnp.exp(scores - jnp.max(scores, axis=-1, keepdims=True))
                prob = scores / jnp.sum(scores, axis=-1, keepdims=True)
                probs[m, h] = prob
                here.append(mm(prob.astype(BF16), value[at]).astype(BF16))
            attended.append(jnp.concatenate(here, axis=1))
        attended = jnp.concatenate(attended, axis=0)
        attended = after(attended, select, select_t, padded_router)
        resid_mid = own + scatter(mm(attended, out_here).astype(BF16))

        def with_other_core(parts):
            arrived = [lax.ppermute(p[1], "core", SWAP) for p in parts]
            return jnp.concatenate(
                [
                    (p[0].astype(F32) + other.astype(F32)).astype(BF16)
                    for p, other in zip(parts, arrived)
                ],
                axis=0,
            )

        moe_scale = norm_scale(resid_mid)
        moe_own = gather_micros((resid_mid * moe_scale * gain_moe).astype(BF16))
        moe_other = [lax.ppermute(rows_here, "core", SWAP) for rows_here in moe_own]
        cot_other = [lax.ppermute(rows_here, "core", SWAP) for rows_here in cot_own]
        saved, out_parts, grad_parts = [], [], []
        for m in micros:
            sets = [slice(0, 2)] if slots <= 288 else [slice(0, 1), slice(1, 2)]
            grads, outs = [], []
            for here in sets:
                grad, out, rest = run_experts(
                    range(2 * m, 2 * m + 2)[here],
                    expert_place,
                    hot,
                    padded_router,
                    select,
                    select_t,
                    [moe_own[m], moe_other[m]][here],
                    [cot_own[m], cot_other[m]][here],
                    w_gate,
                    w_up,
                    w_down,
                    expert_count,
                    hidden,
                )
                grads, outs = grads + list(grad), outs + list(out)
                saved.append(rest)
            grad_parts.append(grads)
            out_parts.append(outs)
        grad_sum = with_other_core(grad_parts)
        grad_moe_in = scatter(grad_sum)

        def over_pairs(left, right):
            total = None
            for rest in saved:
                term = mm_rows(rest[left], rest[right])
                total = term if total is None else total + term
            return total

        def over_x(low, start=None):
            sent = low if start is None else after(low, start)
            return [low] + [
                lax.ppermute(sent, "x", turn(x_count, i)) for i in range(1, x_count)
            ]

        def summed(parts, start):
            parts = [parts[0]] + [after(p, start) for p in parts[1:]]
            if x_count > 2:
                parts = unturn(parts, x_at)
            total = parts[0].astype(F32)
            for item in parts[1:]:
                total = total + item.astype(F32)
            return total.astype(BF16)

        def both_cores(own_part, axis):
            other = lax.ppermute(own_part, "core", SWAP)
            if local_experts == 2:
                return place_experts(core, own_part, other)
            first = jnp.where(core == 0, own_part, other)
            second = jnp.where(core == 0, other, own_part)
            return jnp.concatenate([first, second], axis=axis)[None].astype(F32)

        down_low = over_pairs(2, 1).astype(BF16)
        saved = [[after(r, grad_sum) for r in rest] for rest in saved]
        gate_low = over_pairs(0, 3).astype(BF16)
        up_low = over_pairs(0, 4).astype(BF16)
        router_grad = over_pairs(0, 5)[:, :expert_count]
        down_parts, gate_parts = over_x(down_low), over_x(gate_low)

        grad_out = cotangent.reshape(-1, width).astype(F32)
        moe_gain_grad = jnp.sum(grad_moe_in * resid_mid * moe_scale, axis=0)
        inner = grad_moe_in * gain_moe
        grad_mid = (
            grad_out
            + moe_scale * inner
            - resid_mid * (moe_scale**3 * jnp.mean(resid_mid * inner, axis=-1, keepdims=True))
        )
        grad_attn = gather(grad_mid.astype(BF16))
        mixture = scatter(after(with_other_core(out_parts), grad_attn))
        block_out = (resid_mid + mixture).astype(BF16)
        grad_attended = mm_cols(grad_attn, out_here).astype(BF16)
        down_sum = summed(down_parts, grad_attn)
        up_parts = over_x(up_low, grad_attn)
        grad_query, grad_key, grad_value = [], [], []
        for m in range(micro_count):
            query_here, key_here, value_here = [], [], []
            for h in range(heads_here):
                at = micro_rows(m), head_cols(h)
                prob = probs[m, h]
                value_here.append(mm_rows(prob.astype(BF16), grad_attended[at]).astype(BF16))
                grad_pa = mm_cols(grad_attended[at], value[at])
                delta = jnp.sum(prob * grad_pa, axis=-1, keepdims=True)
                grad_scores = (prob * (grad_pa - delta)).astype(BF16)
                query_here.append(mm(grad_scores, key[at]) * score_scale)
                key_here.append(mm_rows(grad_scores, query[at]) * score_scale)
            grad_query.append(jnp.concatenate(query_here, axis=1))
            grad_key.append(jnp.concatenate(key_here, axis=1))
            grad_value.append(jnp.concatenate(value_here, axis=1))
        grad_query = rope_back(jnp.concatenate(grad_query, axis=0))
        grad_key = rope_back(jnp.concatenate(grad_key, axis=0))
        grad_value = jnp.concatenate(grad_value, axis=0)
        inner_query, inner_key = grad_query * gain_query, grad_key * gain_key
        query_gain_grad = jnp.sum(grad_query * query_raw * query_scale, axis=0)
        key_gain_grad = jnp.sum(grad_key * key_raw * key_scale, axis=0)
        means = jnp.stack(
            [jnp.sum(inner_query * query_raw, axis=1), jnp.sum(inner_key * key_raw, axis=1)]
        )
        means = sum_ep(means, y_count, micro_count) / width
        query_back = (
            query_scale * inner_query - query_raw * (query_scale**3 * means[0][:, None])
        ).astype(BF16)
        key_back = (
            key_scale * inner_key - key_raw * (key_scale**3 * means[1][:, None])
        ).astype(BF16)
        raw_grad = jnp.concatenate([after(query_back, block_out), key_back, grad_value], axis=1)
        d_down = both_cores(down_sum, 0)
        gate_sum = summed(gate_parts, raw_grad)
        normed_part = mm_cols(after(raw_grad, d_down), qkv)
        attn_gain_grad = jnp.sum(normed_part * rows * row_scale, axis=0)
        grad_normed = scatter(normed_part.astype(BF16))
        in_scale = norm_scale(own)
        inner = grad_normed * gain_attn
        d_tokens = (
            grad_mid
            + in_scale * inner
            - own * (in_scale**3 * jnp.mean(own * inner, axis=-1, keepdims=True))
        )

        qkv_grad = mm_rows(normed, raw_grad)
        qkv_kept = keep_core(qkv_grad.reshape(grp_size, -1, 3 * local_width), x_count)
        qkv_grad = keep_x(qkv_kept, x_count, (grad_normed,))
        d_gate = both_cores(gate_sum, 1)
        qkv_grad = after(qkv_grad, d_gate, block_out)
        up_sum = summed(up_parts, grad_normed)
        d_up = both_cores(up_sum, 1)
        qkv_grad = qkv_grad.astype(BF16).reshape(group_size, weight_rows, 3 * local_width)
        qkv_grad = lax.all_to_all(
            qkv_grad, ("z", "y"), split_axis=0, concat_axis=0, tiled=True
        ).astype(F32)

        def by_row(grads):
            shaped = grads.reshape(head_sets, pieces, weight_rows, heads_here, head_dim)
            return shaped.transpose(2, 1, 3, 0, 4).reshape(weight_rows, width)

        d_query = by_row(qkv_grad[:, :, :local_width])
        d_key = by_row(qkv_grad[:, :, local_width : 2 * local_width])
        d_value = by_row(qkv_grad[:, :, 2 * local_width :])
        out_grad = mm_rows(attended, grad_attn)
        out_grad = keep_x(keep_core(out_grad.reshape(grp_size, weight_rows, width), x_count), x_count)
        d_out = lax.ppermute(
            out_grad.astype(BF16), ALL, [(user, home) for home, user in out_pairs]
        ).astype(F32)

        vectors = jnp.stack(
            [
                attn_gain_grad,
                head_part_back(query_gain_grad),
                head_part_back(key_gain_grad),
                moe_gain_grad,
            ]
        )
        vectors = vectors.reshape(4, device_count, weight_rows).transpose(1, 0, 2)
        small_grads = jnp.concatenate(
            [
                vectors.reshape(device_count, 4 * weight_rows),
                router_grad.reshape(device_count, weight_rows * expert_count),
            ],
            axis=1,
        )
        small_grads = lax.all_to_all(
            after(small_grads, grad_normed, gate_sum), ALL, split_axis=0, concat_axis=0, tiled=True
        )
        small_grads = jnp.sum(small_grads, axis=0)
        gain_grads = small_grads[: 4 * weight_rows].reshape(4, weight_rows)
        d_router = small_grads[4 * weight_rows :].reshape(weight_rows, expert_count)

        shape = (micro_count, seq_parts, row_count, width)
        return (
            block_out.reshape(shape),
            d_tokens.reshape(shape),
            gain_grads[0],
            d_query,
            d_key,
            d_value,
            gain_grads[1],
            gain_grads[2],
            d_out,
            gain_grads[3],
            d_router,
            d_gate,
            d_up,
            d_down,
        )

    return per_device


def solution(mesh):
    devices = mesh.devices
    x_count, y_count, z_count = (
        len({device.coords[axis] for device in devices.flat}) for axis in range(3)
    )
    fine = Mesh(devices.reshape(x_count, 2, z_count, y_count), ALL)
    grp, ep = ("x", "core"), ("z", "y")
    by_token = P(None, grp, ep, None)
    vector, matrix, expert = P(ALL), P(ALL, None), P(ep, None, None)
    return jax.shard_map(
        make_per_device(x_count, z_count, y_count),
        mesh=fine,
        in_specs=(
            by_token,
            by_token,
            vector,
            matrix,
            matrix,
            matrix,
            vector,
            vector,
            matrix,
            vector,
            matrix,
            expert,
            expert,
            expert,
            by_token,
        ),
        out_specs=(
            by_token,
            by_token,
            vector,
            matrix,
            matrix,
            matrix,
            vector,
            vector,
            matrix,
            vector,
            matrix,
            expert,
            expert,
            expert,
        ),
        check_vma=False,
    )
```

```python
import functools
import math

import jax
import jax.numpy as jnp
from jax import lax
from jax.experimental import pallas as pl
from jax.experimental.pallas import tpu as pltpu
from jax.sharding import Mesh, PartitionSpec as P

HEADS = 16
CAP = 36
NORM_EPSILON = 1e-05
ROPE_BASE = 10000.0
ALL = ("x", "core", "z", "y")
SWAP = ((0, 1), (1, 0))
F32 = jnp.float32
BF16 = jnp.bfloat16


def turn(count, step):
    return tuple((i, (i + step) % count) for i in range(count))


def flip(count, bits):
    return tuple((i, i ^ bits) for i in range(count))


def after(values, *others):
    if not others:
        return values
    return lax.optimization_barrier((values,) + others)[0]


def mm(left, right):
    return jnp.dot(left, right, preferred_element_type=F32)


def mm_rows(left, right):
    return lax.dot_general(left, right, (((0,), (0,)), ((), ())), preferred_element_type=F32)


def mm_cols(left, right):
    return lax.dot_general(left, right, (((1,), (1,)), ((), ())), preferred_element_type=F32)


def unturn(items, index):
    count = len(items)
    if count == 1:
        return items
    placed = []
    for place in range(count):
        chosen = items[(0 - place) % count]
        for at in range(1, count):
            chosen = jnp.where(index == at, items[(at - place) % count], chosen)
        placed.append(chosen)
    return placed


def gather_ep(block, y_count, micro_count):
    by_z = {0: block}
    by_z[2] = lax.ppermute(block, "z", flip(4, 2))
    by_z[1] = lax.ppermute(block, "z", flip(4, 1))
    blocks = {}

    def along_y(a):
        blocks[a, 0] = by_z[a]
        for j in range(1, y_count):
            blocks[a, j] = lax.ppermute(by_z[a], "y", flip(y_count, j))

    along_y(0)
    by_z[3] = lax.ppermute(by_z[2], "z", flip(4, 1))
    for a in (1, 2, 3):
        along_y(a)
    rows = block.shape[0] // micro_count
    return [
        jnp.concatenate(
            [
                blocks[a, j][m * rows : (m + 1) * rows]
                for a in range(4)
                for j in range(y_count)
            ],
            axis=0,
        )
        for m in range(micro_count)
    ]


def scatter_ep(part, y_count, micro_count, marks=None):
    rows = part.shape[0] // (4 * y_count * micro_count)

    def piece(a, j):
        starts = [((m * 4 + a) * y_count + j) * rows for m in range(micro_count)]
        return jnp.concatenate([part[at : at + rows] for at in starts], axis=0)

    sums = {}

    def along_y(a):
        total = piece(a, 0).astype(F32)
        for j in range(1, y_count):
            arrived = lax.ppermute(piece(a, j).astype(BF16), "y", flip(y_count, j))
            total = total + arrived.astype(F32)
        sums[a] = total

    along_y(3)
    along_y(2)
    sums[2] = sums[2] + lax.ppermute(sums[3].astype(BF16), "z", flip(4, 1)).astype(F32)
    across = lax.ppermute(sums[2].astype(BF16), "z", flip(4, 2)).astype(F32)
    along_y(1)
    if marks is not None:
        marks.append(sums[1])
    near = lax.ppermute(sums[1].astype(BF16), "z", flip(4, 1)).astype(F32)
    along_y(0)
    return sums[0] + near + across


def sum_ep(values, y_count, micro_count):
    shape = values.shape
    values = values.reshape(shape[0] * micro_count, 4, y_count, -1)

    def moved(source, axis, count, at, bits):
        arrived = lax.ppermute(source, axis, flip(count, bits))
        picked = [lax.index_in_dim(arrived, b ^ bits, at, keepdims=True) for b in range(count)]
        return jnp.concatenate(picked, axis=at)

    along = values
    for j in range(1, y_count):
        along = along + moved(values, "y", y_count, 2, j)
    total = along
    for a in (1, 2, 3):
        total = total + moved(along, "z", 4, 1, a)
    return total.reshape(shape)


def gather_grp(block, x_count):
    x_at, core = lax.axis_index("x"), lax.axis_index("core")
    mine = [block] + [lax.ppermute(block, "x", turn(x_count, i)) for i in range(1, x_count)]
    theirs = [lax.ppermute(item, "core", SWAP) for item in mine]
    mine, theirs = unturn(mine, x_at), unturn(theirs, x_at)
    stacked = []
    for own, other in zip(mine, theirs):
        stacked += [jnp.where(core == 0, own, other), jnp.where(core == 0, other, own)]
    return jnp.stack(stacked)


def keep_core(parts, x_count):
    core = lax.axis_index("core")
    parts = parts.reshape((x_count, 2) + parts.shape[1:])
    away = lax.dynamic_index_in_dim(parts, 1 - core, 1, keepdims=False).astype(BF16)
    kept = lax.dynamic_index_in_dim(parts, core, 1, keepdims=False)
    return kept + lax.ppermute(away, "core", SWAP).astype(F32)


def keep_x(kept, x_count, start=()):
    x_at = lax.axis_index("x")
    total = lax.dynamic_index_in_dim(kept, x_at, 0, keepdims=False)
    for i in range(1, x_count):
        away = lax.dynamic_index_in_dim(kept, (x_at - i) % x_count, 0, keepdims=False)
        arrived = lax.ppermute(away.astype(BF16), "x", turn(x_count, -i))
        total = total + after(arrived, *start).astype(F32)
    return total


def experts_kernel(count, which, hot_ref, router_ref, *refs):
    select, select_t, moe, cot = (refs[i * count : (i + 1) * count] for i in range(4))
    gate_ref, up_ref, down_ref = refs[4 * count : 4 * count + 3]
    rest = refs[4 * count + 3 :]
    grad_out, row_out = rest[:count], rest[count : 2 * count]
    rows_ref, cot_ref, act_ref, dgate_ref, dup_ref, logit_ref = rest[2 * count : 2 * count + 6]
    total_ref, back_ref, prob_ref, weight_ref, share_ref = rest[2 * count + 6 :]
    step = pl.program_id(0)
    slots = select[0].shape[1]

    @pl.when(step == 0)
    def _():
        for i in range(count):
            at = pl.ds(i * slots, slots)
            rows_ref[at, :] = mm(select[i][0], moe[i][...]).astype(BF16)
            cot_ref[at, :] = mm(select[i][0], cot[i][...]).astype(BF16)
        logits = mm(rows_ref[...], router_ref[...])
        lane = lax.broadcasted_iota(jnp.int32, logits.shape, 1)
        logits = jnp.where(lane < which, logits, -1e30)
        logits = jnp.exp(logits - jnp.max(logits, axis=1, keepdims=True))
        prob = logits / jnp.sum(logits, axis=1, keepdims=True)
        prob_ref[...] = prob
        weight = jnp.sum(prob * hot_ref[...], axis=1, keepdims=True)
        weight_ref[...] = jnp.broadcast_to(weight, weight_ref.shape)
        share_ref[...] = jnp.zeros_like(share_ref)

    weight = weight_ref[:, :1]
    gate_w, up_w, down_w = gate_ref[0], up_ref[0], down_ref[0]
    gate = mm(rows_ref[...], gate_w)
    up = mm(rows_ref[...], up_w)
    sigmoid = jax.nn.sigmoid(gate)
    silu = gate * sigmoid
    active = silu * up
    act = (weight * active).astype(BF16)
    act_ref[...] = act
    grad = mm_cols(cot_ref[...], down_w)
    share_ref[...] += jnp.broadcast_to(
        jnp.sum(active * grad, axis=1, keepdims=True), share_ref.shape
    )
    grad = weight * grad
    dup = (grad * silu).astype(BF16)
    dgate = (grad * up * (sigmoid + silu * (1.0 - sigmoid))).astype(BF16)
    dup_ref[...] = dup
    dgate_ref[...] = dgate
    weighted = mm(act, down_w)
    back = mm_cols(dgate, gate_w) + mm_cols(dup, up_w)

    @pl.when(step == 0)
    def _():
        total_ref[...] = weighted
        back_ref[...] = back

    @pl.when(step > 0)
    def _():
        total_ref[...] += weighted
        back_ref[...] += back

    @pl.when(step == pl.num_programs(0) - 1)
    def _():
        logit = (share_ref[...] * weight_ref[...] * (hot_ref[...] - prob_ref[...])).astype(BF16)
        logit_ref[...] = logit
        for i in range(count):
            at = pl.ds(i * slots, slots)
            back = (back_ref[at, :] + mm_cols(logit_ref[at, :], router_ref[...])).astype(BF16)
            grad_out[i][...] = mm(select_t[i][0], back).astype(BF16)
            row_out[i][...] = mm(select_t[i][0], total_ref[at, :].astype(BF16)).astype(BF16)


def run_experts(
    sets, at, hot, router, select, select_t, moe, cot, w_gate, w_up, w_down, experts, hidden
):
    count, (slots, seq_len), width = len(sets), select.shape[1:], router.shape[0]
    block = min(hidden, 512)
    steps, rows = hidden // block, count * slots

    def whole(array):
        return pl.BlockSpec(
            array.shape, lambda f, at: (0,) * array.ndim, pipeline_mode=pl.Buffered(1)
        )

    def kept(shape):
        return pl.BlockSpec(shape, lambda f, at: (0, 0), pipeline_mode=pl.Buffered(1))

    wide = pl.BlockSpec((1, width, block), lambda f, at: (at[0], 0, at[1] + f))
    tall = pl.BlockSpec((1, block, width), lambda f, at: (at[0], at[1] + f, 0))
    hidden_rows = pl.BlockSpec((rows, block), lambda f, at: (0, f))
    tables = [array for array in (select, select_t) for _ in sets]
    table_specs = [
        pl.BlockSpec(
            (1,) + array.shape[1:],
            functools.partial(lambda one, f, at: (one, 0, 0), one),
            pipeline_mode=pl.Buffered(1),
        )
        for array in (select, select_t)
        for one in sets
    ]
    one_micro = pl.BlockSpec(
        (seq_len, width), lambda f, at: (micro, 0), pipeline_mode=pl.Buffered(1)
    )
    tables = [array for array in (select, select_t) for _ in sets]
    table_specs = [
        pl.BlockSpec(
            (1,) + array.shape[1:],
            functools.partial(lambda one, f, at: (one, 0, 0), one),
            pipeline_mode=pl.Buffered(1),
        )
        for array in (select, select_t)
        for one in sets
    ]
    tokens = jax.ShapeDtypeStruct((seq_len, width), BF16)
    gathered = jax.ShapeDtypeStruct((rows, width), BF16)
    inner = jax.ShapeDtypeStruct((rows, hidden), BF16)
    result = pl.pallas_call(
        lambda at, *refs: experts_kernel(count, experts, *refs),
        grid_spec=pltpu.PrefetchScalarGridSpec(
            num_scalar_prefetch=1,
            grid=(steps,),
            in_specs=[whole(hot), whole(router)]
            + table_specs
            + [whole(a) for a in (*moe, *cot)]
            + [wide, wide, tall],
            out_specs=[kept((seq_len, width))] * (2 * count)
            + [kept((rows, width))] * 2
            + [hidden_rows] * 3
            + [kept((rows, 128))],
            scratch_shapes=[pltpu.VMEM((rows, width), F32)] * 2
            + [pltpu.VMEM((rows, 128), F32)] * 3,
        ),
        out_shape=[tokens] * (2 * count)
        + [gathered] * 2
        + [inner] * 3
        + [jax.ShapeDtypeStruct((rows, 128), BF16)],
        compiler_params=pltpu.CompilerParams(
            dimension_semantics=("arbitrary",), vmem_limit_bytes=62 * 2**20
        ),
        cost_estimate=pl.CostEstimate(
            flops=12 * rows * hidden * width + 8 * rows * seq_len * width,
            bytes_accessed=6 * hidden * width + 16 * seq_len * width + 8 * rows * width,
            transcendentals=rows * hidden,
        ),
        name="experts",
    )(at, hot, router, *tables, *moe, *cot, w_gate, w_up, w_down)
    return result[:count], result[count : 2 * count], result[2 * count :]


def place_kernel(core_ref, own_ref, other_ref, out_ref):
    @pl.when(core_ref[0] == 0)
    def _():
        out_ref[0] = own_ref[...].astype(F32)
        out_ref[1] = other_ref[...].astype(F32)

    @pl.when(core_ref[0] != 0)
    def _():
        out_ref[0] = other_ref[...].astype(F32)
        out_ref[1] = own_ref[...].astype(F32)


def place_experts(core, own, other):
    rows, columns = own.shape
    block = min(rows, 2**18 // columns)
    half = pl.BlockSpec((block, columns), lambda i, core: (i, 0))
    return pl.pallas_call(
        place_kernel,
        grid_spec=pltpu.PrefetchScalarGridSpec(
            num_scalar_prefetch=1,
            grid=(rows // block,),
            in_specs=[half, half],
            out_specs=pl.BlockSpec((2, block, columns), lambda i, core: (0, i, 0)),
        ),
        out_shape=jax.ShapeDtypeStruct((2, rows, columns), F32),
        compiler_params=pltpu.CompilerParams(
            dimension_semantics=("arbitrary",), vmem_limit_bytes=32 * 2**20
        ),
        cost_estimate=pl.CostEstimate(
            flops=0, bytes_accessed=12 * rows * columns, transcendentals=0
        ),
        name="place",
    )(core[None].astype(jnp.int32), own, other)


def norm_scale(values):
    return lax.rsqrt(jnp.mean(values * values, axis=-1, keepdims=True) + NORM_EPSILON)


def make_per_device(x_count, z_count, y_count):
    group_size = z_count * y_count
    grp_size = 2 * x_count

    assert z_count == 4

    def per_device(
        tokens,
        routes,
        attn_gain,
        w_query,
        w_key,
        w_value,
        query_gain,
        key_gain,
        w_out,
        moe_gain,
        w_router,
        w_gate,
        w_up,
        w_down,
        cotangent,
    ):
        micro_count, seq_parts, row_count, width = tokens.shape
        top_count = routes.shape[3]
        tokens = tokens.reshape(micro_count, row_count, width)
        routes = routes.reshape(micro_count, row_count, top_count)
        cotangent = cotangent.reshape(micro_count, row_count, width)
        expert_count = w_router.shape[1]
        seq_len = row_count * group_size
        head_dim = width // HEADS
        half = head_dim // 2
        score_scale = 1.0 / math.sqrt(head_dim)
        weight_rows = w_query.shape[0]
        pieces = head_dim // weight_rows
        heads_here = grp_size // pieces
        head_sets = group_size // pieces
        local_width = heads_here * head_dim
        x_at, core = lax.axis_index("x"), lax.axis_index("core")
        z_at, y_at = lax.axis_index("z"), lax.axis_index("y")
        ep_at = z_at * y_count + y_at
        set_at, piece_at = ep_at // pieces, ep_at % pieces
        slots = CAP * group_size
        local_experts = w_gate.shape[0]
        ff_width = w_gate.shape[2]

        def gather_micros(block):
            return gather_ep(block.reshape(-1, width), y_count, micro_count)

        def gather(block):
            return jnp.concatenate(gather_micros(block), axis=0)

        def scatter(part, marks=None):
            return scatter_ep(part, y_count, micro_count, marks)

        def by_owner(weight):
            shaped = weight.reshape(weight_rows, pieces, heads_here, head_sets, head_dim)
            return shaped.transpose(3, 1, 0, 2, 4).reshape(group_size, weight_rows, local_width)

        qkv = jnp.concatenate([by_owner(w) for w in (w_query, w_key, w_value)], axis=2)
        qkv = lax.all_to_all(qkv, ("z", "y"), split_axis=0, concat_axis=0, tiled=True)
        small = jnp.concatenate(
            [w_router]
            + [g[:, None] for g in (attn_gain, query_gain, key_gain, moe_gain)],
            axis=1,
        ).reshape(-1)
        naming = jnp.any(
            routes.reshape(1, -1, top_count)
            == jnp.arange(expert_count, dtype=jnp.int32)[:, None, None],
            axis=-1,
        ).astype(BF16)
        if local_experts == 2:
            naming = naming.reshape(group_size, 2, -1).transpose(1, 0, 2)
        else:
            assert local_experts == 1
            naming = jnp.broadcast_to(naming[None], (2,) + naming.shape)
        device_count = grp_size * group_size
        naming = jnp.broadcast_to(naming[None], (x_count,) + naming.shape).reshape(device_count, -1)
        small = jnp.concatenate(
            [jnp.broadcast_to(small[None], (device_count, small.shape[0])), naming], axis=1
        )
        small = lax.all_to_all(after(small, qkv), ALL, split_axis=0, concat_axis=0, tiled=True)
        named = small[:, -micro_count * row_count :]
        small = small[:, : -micro_count * row_count].reshape(width, expert_count + 4)
        full_router = small[:, :expert_count]
        gains = small[:, expert_count:].astype(F32).T
        gain_attn, gain_query, gain_key, gain_moe = gains[0:1], gains[1], gains[2], gains[3:4]

        def head_part(vector):
            shaped = vector.reshape(pieces, heads_here, head_sets, head_dim)
            shaped = lax.dynamic_index_in_dim(shaped, piece_at, 0, keepdims=False)
            return lax.dynamic_index_in_dim(shaped, set_at, 1, keepdims=False).reshape(1, -1)

        def head_part_back(vector):
            piece_hot = jnp.arange(pieces) == piece_at
            set_hot = jnp.arange(head_sets) == set_at
            hot = piece_hot[:, None, None, None] & set_hot[None, None, :, None]
            return jnp.where(hot, vector.reshape(1, heads_here, 1, head_dim), 0.0).reshape(-1)

        gain_query, gain_key = head_part(gain_query), head_part(gain_key)

        sent_qkv = qkv
        qkv = gather_grp(qkv.reshape(group_size * weight_rows, 3 * local_width), x_count)
        qkv = qkv.reshape(width, 3 * local_width)
        out_pairs = []
        for s in range(head_sets):
            for t in range(pieces):
                for h in range(heads_here):
                    for p in range(pieces):
                        home = (t * heads_here + h) * group_size + s * pieces + p
                        user = (h * pieces + p) * group_size + s * pieces + t
                        out_pairs.append((home, user))
        out_here = lax.ppermute(w_out, ALL, out_pairs)
        out_here = gather_grp(out_here, x_count).reshape(local_width, width)

        z_from = z_at ^ jnp.arange(z_count, dtype=jnp.int32)
        y_from = y_at ^ jnp.arange(y_count, dtype=jnp.int32)
        block_from = z_from[:, None] * y_count + y_from[None, :]
        positions = (
            block_from.reshape(-1)[:, None] * row_count
            + jnp.arange(row_count, dtype=jnp.int32)[None, :]
        ).reshape(-1)
        frequency = jnp.exp(
            -math.log(ROPE_BASE) * jnp.arange(half, dtype=F32) * 2.0 / head_dim
        )
        angles = positions.astype(F32)[:, None] * frequency[None, :]
        cosine, sine = jnp.cos(angles), jnp.sin(angles)
        cos_both = jnp.concatenate([cosine, cosine], axis=1)
        sin_both = jnp.concatenate([-sine, sine], axis=1)
        allowed = positions[:, None] >= positions[None, :]

        def halves_swapped(values):
            parts = []
            for h in range(heads_here):
                at = h * head_dim
                parts += [values[:, at + half : at + head_dim], values[:, at : at + half]]
            return jnp.concatenate(parts, axis=1)

        wide_cos = jnp.tile(cos_both, (micro_count, heads_here))
        wide_sin = jnp.tile(sin_both, (micro_count, heads_here))

        def rope(values):
            return values * wide_cos + halves_swapped(values) * wide_sin

        def rope_back(values):
            return values * wide_cos - halves_swapped(values) * wide_sin

        if local_experts == 2:
            expert_at, hidden = ep_at * 2 + core, ff_width
            expert_place = jnp.stack([core, 0 * core]).astype(jnp.int32)
        else:
            expert_at, hidden = ep_at, ff_width // 2
            expert_place = jnp.stack([0 * core, core]).astype(jnp.int32)
        hot = (jnp.arange(128, dtype=jnp.int32) == expert_at).astype(F32)[None]
        padded_router = jnp.pad(full_router, ((0, 0), (0, 128 - expert_count)))

        named = named.reshape((x_count, 2, z_count, y_count, micro_count, row_count))
        named = lax.dynamic_index_in_dim(named, x_at, 0, keepdims=False)
        named = jnp.where(core == 0, named, named[::-1])
        named = jnp.take(jnp.take(named, z_from, axis=1), y_from, axis=2)
        named = named.transpose(3, 0, 1, 2, 4).reshape(2 * micro_count, seq_len) > 0.5
        earlier = jnp.arange(seq_len)[:, None] < jnp.arange(seq_len)[None, :]
        rank = mm(named.astype(BF16), earlier.astype(BF16)).astype(jnp.int32)
        rank = jnp.where(named, rank, -1)
        slot_ids = jnp.arange(slots, dtype=jnp.int32)
        select = (rank[:, None, :] == slot_ids[None, :, None]).astype(BF16)
        select_t = (rank[:, :, None] == slot_ids[None, None, :]).astype(BF16)

        def micro_rows(m):
            return slice(m * seq_len, (m + 1) * seq_len)

        def head_cols(h):
            return slice(h * head_dim, (h + 1) * head_dim)

        own = tokens.reshape(-1, width).astype(F32)
        micros = range(micro_count)
        rows = gather(tokens)
        low_rows = rows
        rows = rows.astype(F32)
        row_scale = norm_scale(rows)
        normed = (rows * row_scale * gain_attn).astype(BF16)
        raw = mm(normed, qkv)
        query_raw, key_raw = raw[:, :local_width], raw[:, local_width : 2 * local_width]
        value = raw[:, 2 * local_width :].astype(BF16)
        squares = jnp.stack(
            [jnp.sum(query_raw * query_raw, axis=1), jnp.sum(key_raw * key_raw, axis=1)]
        )
        squares = sum_ep(squares, y_count, micro_count)
        cot_own = gather_micros(after(cotangent, sent_qkv))
        scales = lax.rsqrt(squares / width + NORM_EPSILON)
        query_scale, key_scale = scales[0][:, None], scales[1][:, None]
        query = rope(query_raw * query_scale * gain_query).astype(BF16)
        key = rope(key_raw * key_scale * gain_key).astype(BF16)
        probs, attended = {}, []
        for m in range(micro_count):
            here = []
            for h in range(heads_here):
                at = micro_rows(m), head_cols(h)
                scores = mm_cols(query[at], key[at]) * score_scale
                scores = jnp.where(allowed, scores, -1e30)
                scores = jnp.exp(scores - jnp.max(scores, axis=-1, keepdims=True))
                prob = scores / jnp.sum(scores, axis=-1, keepdims=True)
                probs[m, h] = prob
                here.append(mm(prob.astype(BF16), value[at]).astype(BF16))
            attended.append(jnp.concatenate(here, axis=1))
        attended = jnp.concatenate(attended, axis=0)
        attended = after(attended, select, select_t, padded_router)
        resid_mid = own + scatter(mm(attended, out_here).astype(BF16))

        def with_other_core(parts):
            arrived = [lax.ppermute(p[1], "core", SWAP) for p in parts]
            return jnp.concatenate(
                [
                    (p[0].astype(F32) + other.astype(F32)).astype(BF16)
                    for p, other in zip(parts, arrived)
                ],
                axis=0,
            )

        moe_scale = norm_scale(resid_mid)
        moe_own = gather_micros((resid_mid * moe_scale * gain_moe).astype(BF16))
        moe_other = [lax.ppermute(rows_here, "core", SWAP) for rows_here in moe_own]
        cot_other = [lax.ppermute(rows_here, "core", SWAP) for rows_here in cot_own]
        saved, out_parts, grad_parts = [], [], []
        for m in micros:
            sets = [slice(0, 2)] if slots <= 288 else [slice(0, 1), slice(1, 2)]
            grads, outs = [], []
            for here in sets:
                grad, out, rest = run_experts(
                    range(2 * m, 2 * m + 2)[here],
                    expert_place,
                    hot,
                    padded_router,
                    select,
                    select_t,
                    [moe_own[m], moe_other[m]][here],
                    [cot_own[m], cot_other[m]][here],
                    w_gate,
                    w_up,
                    w_down,
                    expert_count,
                    hidden,
                )
                grads, outs = grads + list(grad), outs + list(out)
                saved.append(rest)
            grad_parts.append(grads)
            out_parts.append(outs)
        grad_sum = with_other_core(grad_parts)
        grad_moe_in = scatter(grad_sum)

        def over_pairs(left, right):
            total = None
            for rest in saved:
                term = mm_rows(rest[left], rest[right])
                total = term if total is None else total + term
            return total

        def over_x(low, start=None):
            sent = low if start is None else after(low, start)
            return [low] + [
                lax.ppermute(sent, "x", turn(x_count, i)) for i in range(1, x_count)
            ]

        def summed(parts, start):
            parts = [parts[0]] + [after(p, start) for p in parts[1:]]
            if x_count > 2:
                parts = unturn(parts, x_at)
            total = parts[0].astype(F32)
            for item in parts[1:]:
                total = total + item.astype(F32)
            return total.astype(BF16)

        def both_cores(own_part, axis):
            other = lax.ppermute(own_part, "core", SWAP)
            if local_experts == 2:
                return place_experts(core, own_part, other)
            first = jnp.where(core == 0, own_part, other)
            second = jnp.where(core == 0, other, own_part)
            return jnp.concatenate([first, second], axis=axis)[None].astype(F32)

        down_low = over_pairs(2, 1).astype(BF16)
        saved = [[after(r, grad_sum) for r in rest] for rest in saved]
        gate_low = over_pairs(0, 3).astype(BF16)
        up_low = over_pairs(0, 4).astype(BF16)
        router_grad = over_pairs(0, 5)[:, :expert_count]
        down_parts, gate_parts = over_x(down_low), over_x(gate_low)

        grad_out = cotangent.reshape(-1, width).astype(F32)
        moe_gain_grad = jnp.sum(grad_moe_in * resid_mid * moe_scale, axis=0)
        inner = grad_moe_in * gain_moe
        grad_mid = (
            grad_out
            + moe_scale * inner
            - resid_mid * (moe_scale**3 * jnp.mean(resid_mid * inner, axis=-1, keepdims=True))
        )
        grad_attn = gather(grad_mid.astype(BF16))
        mixture = scatter(after(with_other_core(out_parts), grad_attn))
        block_out = (resid_mid + mixture).astype(BF16)
        grad_attended = mm_cols(grad_attn, out_here).astype(BF16)
        down_sum = summed(down_parts, grad_attn)
        up_parts = over_x(up_low, grad_attn)
        grad_query, grad_key, grad_value = [], [], []
        for m in range(micro_count):
            query_here, key_here, value_here = [], [], []
            for h in range(heads_here):
                at = micro_rows(m), head_cols(h)
                prob = probs[m, h]
                value_here.append(mm_rows(prob.astype(BF16), grad_attended[at]).astype(BF16))
                grad_pa = mm_cols(grad_attended[at], value[at])
                delta = jnp.sum(prob * grad_pa, axis=-1, keepdims=True)
                grad_scores = (prob * (grad_pa - delta)).astype(BF16)
                query_here.append(mm(grad_scores, key[at]) * score_scale)
                key_here.append(mm_rows(grad_scores, query[at]) * score_scale)
            grad_query.append(jnp.concatenate(query_here, axis=1))
            grad_key.append(jnp.concatenate(key_here, axis=1))
            grad_value.append(jnp.concatenate(value_here, axis=1))
        grad_query = rope_back(jnp.concatenate(grad_query, axis=0))
        grad_key = rope_back(jnp.concatenate(grad_key, axis=0))
        grad_value = jnp.concatenate(grad_value, axis=0)
        inner_query, inner_key = grad_query * gain_query, grad_key * gain_key
        query_gain_grad = jnp.sum(grad_query * query_raw * query_scale, axis=0)
        key_gain_grad = jnp.sum(grad_key * key_raw * key_scale, axis=0)
        means = jnp.stack(
            [jnp.sum(inner_query * query_raw, axis=1), jnp.sum(inner_key * key_raw, axis=1)]
        )
        means = sum_ep(means, y_count, micro_count) / width
        query_back = (
            query_scale * inner_query - query_raw * (query_scale**3 * means[0][:, None])
        ).astype(BF16)
        key_back = (
            key_scale * inner_key - key_raw * (key_scale**3 * means[1][:, None])
        ).astype(BF16)
        raw_grad = jnp.concatenate([after(query_back, block_out), key_back, grad_value], axis=1)
        d_down = both_cores(down_sum, 0)
        gate_sum = summed(gate_parts, raw_grad)
        normed_part = mm_cols(after(raw_grad, d_down), qkv)
        attn_gain_grad = jnp.sum(normed_part * rows * row_scale, axis=0)
        marks = []
        grad_normed = scatter(normed_part.astype(BF16), marks)
        in_scale = norm_scale(own)
        inner = grad_normed * gain_attn
        d_tokens = (
            grad_mid
            + in_scale * inner
            - own * (in_scale**3 * jnp.mean(own * inner, axis=-1, keepdims=True))
        )

        qkv_grad = mm_rows(normed, raw_grad)
        qkv_kept = keep_core(qkv_grad.reshape(grp_size, -1, 3 * local_width), x_count)
        qkv_grad = keep_x(qkv_kept, x_count, marks)
        d_gate = both_cores(gate_sum, 1)
        qkv_grad = after(qkv_grad, d_gate, block_out)
        up_sum = summed(up_parts, grad_normed)
        d_up = both_cores(up_sum, 1)
        qkv_grad = qkv_grad.astype(BF16).reshape(group_size, weight_rows, 3 * local_width)
        qkv_grad = lax.all_to_all(
            qkv_grad, ("z", "y"), split_axis=0, concat_axis=0, tiled=True
        ).astype(F32)

        def by_row(grads):
            shaped = grads.reshape(head_sets, pieces, weight_rows, heads_here, head_dim)
            return shaped.transpose(2, 1, 3, 0, 4).reshape(weight_rows, width)

        d_query = by_row(qkv_grad[:, :, :local_width])
        d_key = by_row(qkv_grad[:, :, local_width : 2 * local_width])
        d_value = by_row(qkv_grad[:, :, 2 * local_width :])
        out_grad = mm_rows(attended, grad_attn)
        out_grad = keep_x(keep_core(out_grad.reshape(grp_size, weight_rows, width), x_count), x_count)
        d_out = lax.ppermute(
            out_grad.astype(BF16), ALL, [(user, home) for home, user in out_pairs]
        ).astype(F32)

        vectors = jnp.stack(
            [
                attn_gain_grad,
                head_part_back(query_gain_grad),
                head_part_back(key_gain_grad),
                moe_gain_grad,
            ]
        )
        vectors = vectors.reshape(4, device_count, weight_rows).transpose(1, 0, 2)
        small_grads = jnp.concatenate(
            [
                vectors.reshape(device_count, 4 * weight_rows),
                router_grad.reshape(device_count, weight_rows * expert_count),
            ],
            axis=1,
        )
        small_grads = lax.all_to_all(
            after(small_grads, grad_normed, gate_sum), ALL, split_axis=0, concat_axis=0, tiled=True
        )
        small_grads = jnp.sum(small_grads, axis=0)
        gain_grads = small_grads[: 4 * weight_rows].reshape(4, weight_rows)
        d_router = small_grads[4 * weight_rows :].reshape(weight_rows, expert_count)

        shape = (micro_count, seq_parts, row_count, width)
        return (
            block_out.reshape(shape),
            d_tokens.reshape(shape),
            gain_grads[0],
            d_query,
            d_key,
            d_value,
            gain_grads[1],
            gain_grads[2],
            d_out,
            gain_grads[3],
            d_router,
            d_gate,
            d_up,
            d_down,
        )

    return per_device


def solution(mesh):
    devices = mesh.devices
    x_count, y_count, z_count = (
        len({device.coords[axis] for device in devices.flat}) for axis in range(3)
    )
    fine = Mesh(devices.reshape(x_count, 2, z_count, y_count), ALL)
    grp, ep = ("x", "core"), ("z", "y")
    by_token = P(None, grp, ep, None)
    vector, matrix, expert = P(ALL), P(ALL, None), P(ep, None, None)
    return jax.shard_map(
        make_per_device(x_count, z_count, y_count),
        mesh=fine,
        in_specs=(
            by_token,
            by_token,
            vector,
            matrix,
            matrix,
            matrix,
            vector,
            vector,
            matrix,
            vector,
            matrix,
            expert,
            expert,
            expert,
            by_token,
        ),
        out_specs=(
            by_token,
            by_token,
            vector,
            matrix,
            matrix,
            matrix,
            vector,
            vector,
            matrix,
            vector,
            matrix,
            expert,
            expert,
            expert,
        ),
        check_vma=False,
    )
```
